32 devices in a mesh: groups: 1, expert: 32 (over z, y, x, core).
Axes of the slice: x: 2, y: 2, z: 4, core: 2. Of those that a mesh axis runs over, the one named last changes fastest.
Arguments:
- tokens: bfloat16 [2048, 4096], P(('groups', 'expert')), may hold values from -6 to 6
- route_ids: int32 [2048, 8], P(('groups', 'expert')), may hold values from 0 to 15, all different within a row; in each aligned block of 64 rows (0 to 63, 64 to 127, ...) at most 40 rows name the same one
- route_gates: float32 [2048, 8], P(('groups', 'expert')), may hold values from 0.05 to 1
- gate_weight: bfloat16 [4096, 12288], P(None, 'expert'), may hold values from -0.09375 to 0.09375
- up_weight: bfloat16 [4096, 12288], P(None, 'expert'), may hold values from -0.09375 to 0.09375
- down_weight: bfloat16 [12288, 4096], P('expert'), may hold values from -0.4375 to 0.4375
- kv_pages: bfloat16 [1024, 16, 1024], P(('groups', 'expert')), may hold values from -6 to 6
- page_target: int32 [1024], P(('groups', 'expert')), may hold values from 0 to 1023, as said below
Outputs:
- combined: bfloat16 [2048, 4096], P(('groups', 'expert'))
- handed_pages: bfloat16 [1024, 16, 1024], P(('groups', 'expert'))
The draws below stay inside these ranges and needn't reach their ends.
Inputs may be any that keep to these rules, and one draw needn't show every extreme that they name: `route_ids`: each row names 8 different experts; the rows of one device name one expert at most 40 times, a bound that some block reaches. A permutation; page p goes to device page_target[p] // 32. Every device receives exactly 32 pages, at most 1 of them from one device and exactly 1 from some device; the distances from source to destination device, modulo the axis, form the same multiset on every device.
All inputs are finite; a program needn't handle non-finite values.
Results may differ from the reference program's by a relative error of at most 0.0064.
Values may be sent and summed in bfloat16 or wider, within the bound.
No kernel may reach another device: no remote copies, remote signals or barrier semaphores. Data moves between devices by JAX's collectives and lax.ppermute only.
A program may use at most 128 MiB of HBM per device.

```python
import math
import jax
import jax.numpy as jnp
import numpy as np
from jax import lax

D = 4096
FF = 768
TOP = 8
PAGE_TOK = 16
KVW = 1024
PCAP = 1
TOK_DEV = 64
PAGES_DEV = 32
EXPERTS = 16
CAP = 40
TOKENS = 2048
PAGES = 1024
N_EXPERT = 32


def draw_page_target(key, part):
    key = jax.random.fold_in(key, 7)
    keys = jax.random.split(key, 4)
    spots = jnp.arange(N_EXPERT, dtype=jnp.int32)
    ranking = jax.random.permutation(keys[0], N_EXPERT).astype(jnp.int32)
    ranking = jnp.where(spots == 1, -2, jnp.where(spots == N_EXPERT // 2, -1, ranking))
    distinct = jnp.argsort(ranking).astype(jnp.int32)[:PAGES_DEV - PCAP + 1]
    offsets = jnp.concatenate([jnp.full((PCAP - 1,), distinct[0], jnp.int32), distinct.astype(jnp.int32)])
    offsets = jax.random.permutation(keys[1], offsets)
    sender_order = jax.vmap(lambda k: jax.random.permutation(k, PAGES_DEV))(jax.random.split(keys[2], N_EXPERT))
    receiver_order = jax.vmap(lambda k: jax.random.permutation(k, PAGES_DEV))(jax.random.split(keys[3], N_EXPERT))
    sender = jnp.arange(N_EXPERT, dtype=jnp.int32)[:, None]
    receiver = (sender + offsets[sender_order]) % N_EXPERT
    place = receiver_order[receiver, sender_order]
    return (receiver * PAGES_DEV + place).reshape(-1).astype(jnp.int32)


def levels(key, dims, pieces, low, high):
    level, own = 1.0, jax.random.fold_in(key, 6)
    for dim, blocks in pieces:
        heights = jnp.exp(jax.random.uniform(jax.random.fold_in(own, dim), (blocks,), jnp.float32, low / len(pieces), high / len(pieces)))
        level = level * jnp.repeat(heights, dims[dim] // blocks).reshape([-1 if axis == dim else 1 for axis in range(len(dims))])
    return level


def shared_out(stream_key, own, number, rows, number_of, top, most, lean):
    sequence = jax.random.permutation(stream_key, number_of)
    crowded, usual = load_shares(number_of, rows * top, most, lean, True), load_shares(number_of, rows * top, most, lean, False)
    places = jnp.arange(number_of)

    def named(sizes, offset_by):
        used = int((sizes > 0).sum())
        fixed = max(1, used // 4)
        shifted = fixed + (places - fixed + offset_by * (used - fixed)) % max(1, number_of - fixed)
        return jnp.zeros((number_of,), jnp.int32).at[sequence[jnp.where(places < fixed, places, shifted)]].set(jnp.asarray(sizes, jnp.int32))

    sizes = jnp.where(number % 4 == 0, named(crowded, number // 4), named(usual, number - number // 4 - 1))
    mixed = jax.random.permutation(jax.random.fold_in(own, 3), number_of)
    source_of, sink = mixed[0:number_of // 2 * 2:2], mixed[1:number_of // 2 * 2:2]
    room = jnp.minimum(sizes[source_of] - 1, most - sizes[sink]) // 2
    room = jnp.where((source_of == sequence[0]) | (sink == sequence[0]) | (sizes[sink] == 0), 0, jnp.maximum(room, 0))
    shifted = jax.random.randint(jax.random.fold_in(own, 4), (number_of // 2,), 0, 1 << 20) % (room + 1)
    sizes = sizes.at[source_of].add(-shifted).at[sink].add(shifted)
    items = jnp.searchsorted(jnp.cumsum(sizes), jnp.arange(rows * top), side="right").astype(jnp.int32)
    listing = items.reshape(top, rows).T
    listing = listing[jax.random.permutation(jax.random.fold_in(own, 1), rows)]
    offset_by = jax.random.randint(jax.random.fold_in(own, 2), (rows, 1), 0, top)
    return jnp.take_along_axis(listing, (jnp.arange(top)[None, :] + offset_by) % top, axis=1)


def load_shares(count, total, most, skew, full):
    portions = [(1 << 20) // math.isqrt(standing ** skew) + 1 for standing in range(1, count + 1)]
    largest = most if full else min(most, max(-(-total // count), total * portions[0] // sum(portions)))
    least = 1 if total - largest >= count - 1 else 0
    given, rest = [largest] + [least] * (count - 1), total - largest - least * (count - 1)
    while rest > 0:
        candidates = [i for i in range(1, count) if given[i] < largest] or [i for i in range(1, count) if given[i] < most]
        mass, remaining = sum([portions[i] for i in candidates]), rest
        for i in candidates:
            more = min(most - given[i], max(1, remaining * portions[i] // mass), rest)
            given[i] = given[i] + more
            rest = rest - more
    return np.array(given)


def normal_values(stream_key, extent, width, reach, pieces=(), kind=jnp.bfloat16):
    result = jax.random.normal(stream_key, extent, jnp.float32) * width
    if len(pieces) > 0:
        result = levels(stream_key, extent, pieces, -0.22, 0.18) * result
    return jnp.clip(result, min=-reach, max=reach).astype(kind)


def setup_inputs(seed: int = 0, part: int = 0) -> dict:
    key_of = jax.random.split(jax.random.key(seed), 9)
    own_keys = jax.random.split(jax.random.fold_in(key_of[8], part), 9)
    tokens = normal_values(own_keys[0], (TOKENS, D), 1.0, 6.0, ((0, 32),))
    route_ids_keys = jax.random.split(jax.random.fold_in(own_keys[1], 1), TOKENS // TOK_DEV)
    route_ids_turns = jax.random.permutation(jax.random.fold_in(own_keys[1], 3), TOKENS // TOK_DEV)
    route_ids = jax.vmap(lambda own, number: shared_out(jax.random.fold_in(own_keys[1], 2), own, number, TOK_DEV, EXPERTS, TOP, CAP, 2))(route_ids_keys, route_ids_turns).reshape((TOKENS, TOP))
    route_gates = jnp.clip(jnp.exp(math.log(1.0) - 2.9957323 * jax.random.uniform(own_keys[2], (TOKENS, TOP), jnp.float32) ** levels(own_keys[2], (TOKENS, TOP), ((0, 32),), -0.2, 0.2)), 0.05, 1.0)
    gate_weight = normal_values(key_of[3], (D, EXPERTS * FF), D ** -0.5, 0.09375, ((1, 32),))
    up_weight = normal_values(key_of[4], (D, EXPERTS * FF), D ** -0.5, 0.09375, ((1, 32),))
    down_weight = normal_values(key_of[5], (EXPERTS * FF, D), (FF // 4) ** -0.5, 0.4375, ((0, 32),))
    kv_pages = normal_values(own_keys[6], (PAGES, PAGE_TOK, KVW), 1.0, 6.0, ((0, 32),))
    page_target = draw_page_target(jax.random.fold_in(jax.random.fold_in(key_of[8], part), 71), part)
    return dict(tokens=tokens, route_ids=route_ids, route_gates=route_gates, gate_weight=gate_weight, up_weight=up_weight, down_weight=down_weight, kv_pages=kv_pages, page_target=page_target)


def expert_apply(rows, gate_cols, up_cols, down_rows):
    gate = jnp.dot(rows, gate_cols, preferred_element_type=jnp.float32)
    up = jnp.dot(rows, up_cols, preferred_element_type=jnp.float32)
    hidden = (jax.nn.silu(gate) * up).astype(jnp.bfloat16)
    return jnp.dot(hidden, down_rows, preferred_element_type=jnp.float32).astype(jnp.bfloat16)


def reference(tokens, route_ids, route_gates, gate_weight, up_weight, down_weight, kv_pages, page_target):
    shares = route_gates / jnp.sum(route_gates, axis=1, keepdims=True)
    mixing = shares.astype(jnp.bfloat16)
    per_device = route_ids.reshape(N_EXPERT, TOK_DEV * TOP)
    onehot = (per_device[:, :, None] == jnp.arange(EXPERTS, dtype=jnp.int32)[None, None, :]).astype(jnp.int32)
    earlier = jnp.cumsum(onehot, axis=1) - onehot
    slots = jnp.sum(earlier * onehot, axis=2).astype(jnp.int32)
    source = jnp.arange(N_EXPERT, dtype=jnp.int32)[:, None]
    where_to = ((per_device * N_EXPERT + source) * CAP + slots).reshape(-1).astype(jnp.int32)
    token_of = (jnp.arange(TOKENS * TOP, dtype=jnp.int32) // TOP).astype(jnp.int32)
    table = jnp.zeros((EXPERTS * N_EXPERT * CAP,), jnp.int32).at[where_to].set(token_of)
    weight_table = jnp.zeros((EXPERTS * N_EXPERT * CAP,), jnp.float32).at[where_to].set(mixing.reshape(-1).astype(jnp.float32))
    table = table.reshape(EXPERTS, N_EXPERT * CAP)
    weight_table = weight_table.reshape(EXPERTS, N_EXPERT * CAP)

    def visit(total, expert):
        picks = table[expert]
        blend = weight_table[expert]
        rows = tokens[picks]
        start = (expert * FF).astype(jnp.int32)
        gate_cols = lax.dynamic_slice_in_dim(gate_weight, start, FF, 1)
        up_cols = lax.dynamic_slice_in_dim(up_weight, start, FF, 1)
        down_rows = lax.dynamic_slice_in_dim(down_weight, start, FF, 0)
        out_rows = expert_apply(rows, gate_cols, up_cols, down_rows)
        total = total.at[picks].add(blend[:, None] * out_rows.astype(blend.dtype))
        return total, None

    total, _ = lax.scan(visit, jnp.zeros((TOKENS, D), jnp.float32), jnp.arange(EXPERTS, dtype=jnp.int32))
    handed = jnp.zeros_like(kv_pages).at[page_target].set(kv_pages)
    return (total.astype(jnp.bfloat16), handed)
```

```python
import jax
import jax.numpy as jnp
from jax import lax
from jax.sharding import PartitionSpec as P

PCAP = 1
PLANE = 4


def slot_ranks(labels, count):
    onehot = (labels[:, None] == jnp.arange(count, dtype=jnp.int32)[None, :]).astype(jnp.int32)
    earlier = jnp.cumsum(onehot, axis=0) - onehot
    return jnp.sum(earlier * onehot, axis=1)


def place_pages(arrived, arrived_labels, page_count, page_shape):
    picking = (
        arrived_labels.astype(jnp.float32)[None, :]
        == jnp.arange(page_count, dtype=jnp.float32)[:, None]
    ).astype(jnp.bfloat16)
    landed = jnp.dot(picking, arrived, preferred_element_type=jnp.float32)
    return landed.astype(jnp.bfloat16).reshape(page_shape)


def hand_pages(kv_pages, page_target):
    page_count = kv_pages.shape[0]
    owners = lax.axis_size("expert")
    target_dev = page_target // page_count
    target_slot = page_target % page_count
    flat_pages = kv_pages.reshape(page_count, -1)
    position = target_dev * PCAP + slot_ranks(target_dev, owners)
    placing = position[:, None] == jnp.arange(owners * PCAP, dtype=jnp.int32)[None, :]
    outgoing = lax.dot_general(
        placing.astype(jnp.bfloat16),
        flat_pages,
        (((0,), (0,)), ((), ())),
        preferred_element_type=jnp.float32,
    ).astype(jnp.bfloat16)
    labels = jnp.sum(jnp.where(placing, target_slot[:, None] + 1, 0), axis=0) - 1
    arrived, arrived_labels = (
        lax.all_to_all(outgoing, "expert", split_axis=0, concat_axis=0, tiled=True),
        lax.all_to_all(
            labels.astype(jnp.bfloat16), "expert", split_axis=0, concat_axis=0, tiled=True
        ),
    )
    return place_pages(arrived, arrived_labels, page_count, kv_pages.shape)


def send(x, step=None, flip=None):
    count = lax.axis_size("expert")
    if flip is not None:
        pairs = [(i, i ^ flip) for i in range(count)]
    else:
        pairs = [(i, (i + step) % count) for i in range(count)]
    return lax.ppermute(x, "expert", pairs)


def mixing_table(route_ids, route_gates, experts):
    shares = route_gates / jnp.sum(route_gates, axis=1, keepdims=True)
    mixing = shares.astype(jnp.bfloat16).astype(jnp.float32)
    hits = route_ids[:, :, None] == jnp.arange(experts, dtype=jnp.int32)
    return jnp.sum(jnp.where(hits, mixing[:, :, None], 0.0), axis=1).astype(jnp.bfloat16)


def plane_slots(table, nearby, capacity):
    rows = table.shape[0]
    weight = jnp.dot(table, nearby, preferred_element_type=jnp.float32)
    named = weight > 0
    below = jnp.arange(rows)[:, None] > jnp.arange(rows)[None, :]
    rank = jnp.dot(
        below.astype(jnp.bfloat16), named.astype(jnp.bfloat16), preferred_element_type=jnp.float32
    )
    hits = (rank[:, :, None] == jnp.arange(capacity, dtype=jnp.float32)) & named[:, :, None]
    placing = hits.astype(jnp.bfloat16)
    blend = jnp.where(hits, weight[:, :, None], 0.0).astype(jnp.bfloat16)
    return placing, blend


def local(
    tokens, route_ids, route_gates, gate_weight, up_weight, down_weight, kv_pages, page_target
):
    tok_rows, width = tokens.shape
    chosen = route_ids.shape[1]
    owners = lax.axis_size("expert")
    experts = owners // 2
    planes = experts // PLANE
    stride = 2 * PLANE
    capacity = min(tok_rows, 5 * tok_rows * chosen // (4 * experts))
    chip = lax.axis_index("expert") // 2
    near = (chip // PLANE) * PLANE + ((chip % PLANE) ^ jnp.arange(PLANE, dtype=jnp.int32))
    nearby = (jnp.arange(experts, dtype=jnp.int32)[:, None] == near[None, :]).astype(jnp.bfloat16)

    blocks = [tokens]
    for _ in range(1, planes):
        blocks.append(send(blocks[-1], step=stride))
    table = mixing_table(route_ids, route_gates, experts)
    tables = [table] + [send(table, step=stride * s) for s in range(1, planes)]

    gate_all = jnp.concatenate([gate_weight, send(gate_weight, flip=1)], axis=1)
    up_all = jnp.concatenate([up_weight, send(up_weight, flip=1)], axis=1)
    down_all = jnp.concatenate([down_weight, send(down_weight, flip=1)], axis=0)

    held, blends = [], []
    for s in range(planes):
        placing, blend = plane_slots(tables[s], nearby, capacity)
        blends.append(blend.reshape(tok_rows, PLANE * capacity))
        for j in range(PLANE):
            picked = lax.dot_general(
                placing[:, j],
                blocks[s],
                (((0,), (0,)), ((), ())),
                preferred_element_type=jnp.float32,
            ).astype(jnp.bfloat16)
            held.append(send(picked, flip=2 * j) if j else picked)

    outs = []
    group = 2
    for first in range(0, planes, group):
        rows = jnp.concatenate(held[first * PLANE : (first + group) * PLANE], axis=0)
        gate = jnp.dot(rows, gate_all, preferred_element_type=jnp.float32)
        up = jnp.dot(rows, up_all, preferred_element_type=jnp.float32)
        hidden = (jax.nn.silu(gate) * up).astype(jnp.bfloat16)
        out = jnp.dot(hidden, down_all, preferred_element_type=jnp.float32).astype(jnp.bfloat16)
        outs.extend(jnp.split(out, group * PLANE, axis=0))

    def returned(s):
        mine = outs[s * PLANE : (s + 1) * PLANE]
        back = [mine[0]] + [send(mine[j], flip=2 * j) for j in range(1, PLANE)]
        return jnp.dot(
            blends[s], jnp.concatenate(back, axis=0), preferred_element_type=jnp.float32
        )

    total = returned(1).astype(jnp.bfloat16)
    for s in list(range(2, planes)) + [0]:
        arrived = send(total, step=stride)
        total = (returned(s) + arrived.astype(jnp.float32)).astype(jnp.bfloat16)
    handed = hand_pages(kv_pages, page_target)
    return (total, handed)


def solution(mesh):
    placed = (
        P(("groups", "expert"), None),
        P(("groups", "expert"), None),
        P(("groups", "expert"), None),
        P(None, "expert"),
        P(None, "expert"),
        P("expert", None),
        P(("groups", "expert"), None, None),
        P(("groups", "expert")),
    )
    return jax.shard_map(
        local,
        mesh=mesh,
        in_specs=placed,
        out_specs=(P(("groups", "expert"), None), P(("groups", "expert"), None, None)),
        check_vma=False,
    )
```

```python
import jax
import jax.numpy as jnp
from jax import lax
from jax.sharding import PartitionSpec as P

PCAP = 1
PLANE = 4


def slot_ranks(labels, count):
    onehot = (labels[:, None] == jnp.arange(count, dtype=jnp.int32)[None, :]).astype(jnp.int32)
    earlier = jnp.cumsum(onehot, axis=0) - onehot
    return jnp.sum(earlier * onehot, axis=1)


def place_pages(arrived, arrived_labels, page_count, page_shape):
    picking = (
        arrived_labels.astype(jnp.float32)[None, :]
        == jnp.arange(page_count, dtype=jnp.float32)[:, None]
    ).astype(jnp.bfloat16)
    landed = jnp.dot(picking, arrived, preferred_element_type=jnp.float32)
    return landed.astype(jnp.bfloat16).reshape(page_shape)


def hand_pages(kv_pages, page_target, earlier):
    page_count = kv_pages.shape[0]
    owners = lax.axis_size("expert")
    target_dev = page_target // page_count
    target_slot = page_target % page_count
    flat_pages = kv_pages.reshape(page_count, -1)
    position = target_dev * PCAP + slot_ranks(target_dev, owners)
    placing = position[:, None] == jnp.arange(owners * PCAP, dtype=jnp.int32)[None, :]
    outgoing = lax.dot_general(
        placing.astype(jnp.bfloat16),
        flat_pages,
        (((0,), (0,)), ((), ())),
        preferred_element_type=jnp.float32,
    ).astype(jnp.bfloat16)
    labels = jnp.sum(jnp.where(placing, target_slot[:, None] + 1, 0), axis=0) - 1
    arrived, arrived_labels = (
        lax.all_to_all(after(outgoing, earlier), "expert", split_axis=0, concat_axis=0, tiled=True),
        lax.all_to_all(
            labels.astype(jnp.bfloat16), "expert", split_axis=0, concat_axis=0, tiled=True
        ),
    )
    return place_pages(arrived, arrived_labels, page_count, kv_pages.shape)


def send(x, step=None, flip=None):
    count = lax.axis_size("expert")
    if flip is not None:
        pairs = [(i, i ^ flip) for i in range(count)]
    else:
        pairs = [(i, (i + step) % count) for i in range(count)]
    return lax.ppermute(x, "expert", pairs)


def after(x, *earlier):
    return lax.optimization_barrier((x, *earlier))[0]


def mixing_table(route_ids, route_gates, experts):
    shares = route_gates / jnp.sum(route_gates, axis=1, keepdims=True)
    mixing = shares.astype(jnp.bfloat16).astype(jnp.float32)
    hits = route_ids[:, :, None] == jnp.arange(experts, dtype=jnp.int32)
    return jnp.sum(jnp.where(hits, mixing[:, :, None], 0.0), axis=1).astype(jnp.bfloat16)


def plane_slots(table, nearby, capacity):
    rows = table.shape[0]
    weight = jnp.dot(table, nearby, preferred_element_type=jnp.float32)
    named = weight > 0
    below = jnp.arange(rows)[:, None] > jnp.arange(rows)[None, :]
    rank = jnp.dot(
        below.astype(jnp.bfloat16), named.astype(jnp.bfloat16), preferred_element_type=jnp.float32
    )
    hits = (rank[:, :, None] == jnp.arange(capacity, dtype=jnp.float32)) & named[:, :, None]
    placing = hits.astype(jnp.bfloat16)
    blend = jnp.where(hits, weight[:, :, None], 0.0).astype(jnp.bfloat16)
    return placing, blend


def apply(held, gate_weight, up_weight, down_weight):
    pieces = [piece for arrived in held for piece in arrived]
    rows = jnp.concatenate(pieces, axis=0)
    gate = jnp.dot(rows, gate_weight, preferred_element_type=jnp.float32)
    up = jnp.dot(rows, up_weight, preferred_element_type=jnp.float32)
    hidden = lax.optimization_barrier((jax.nn.silu(gate) * up).astype(jnp.bfloat16))
    out = jnp.dot(hidden, down_weight, preferred_element_type=jnp.float32)
    return jnp.split(out.astype(jnp.bfloat16), len(pieces), axis=0)


def local(
    tokens, route_ids, route_gates, gate_weight, up_weight, down_weight, kv_pages, page_target
):
    tok_rows, width = tokens.shape
    chosen = route_ids.shape[1]
    owners = lax.axis_size("expert")
    experts = owners // 2
    planes = experts // PLANE
    stride = 2 * PLANE
    capacity = min(tok_rows, 5 * tok_rows * chosen // (4 * experts))
    chip = lax.axis_index("expert") // 2
    near = (chip // PLANE) * PLANE + ((chip % PLANE) ^ jnp.arange(PLANE, dtype=jnp.int32))
    nearby = (jnp.arange(experts, dtype=jnp.int32)[:, None] == near[None, :]).astype(jnp.bfloat16)

    table = mixing_table(route_ids, route_gates, experts)
    lanes = jnp.pad(table, ((0, 0), (0, -experts % 128)))
    block = jnp.concatenate([tokens, lanes], axis=1)
    weights = (gate_weight, up_weight, down_weight)
    group = 2
    swapped, blends, got, outs = [], [], [], []
    for s in range(planes):
        placing, blend = plane_slots(block[:, width : width + experts], nearby, capacity)
        blends.append(blend.reshape(tok_rows, PLANE * capacity))
        if s < 3:
            swapped.append(send(after(weights[s], *swapped), flip=1))
        arrived = []
        for j in range(PLANE):
            picked = lax.dot_general(
                placing[:, j],
                block[:, :width],
                (((0,), (0,)), ((), ())),
                preferred_element_type=jnp.float32,
            ).astype(jnp.bfloat16)
            if j:
                if s:
                    picked = after(picked, got[s - 1][j])
                picked = send(picked, flip=2 * j)
            arrived.append(picked)
        if s + 1 < planes:
            block = send(block, step=stride)
        got.append(arrived)
    gate_all = jnp.concatenate([gate_weight, swapped[0]], axis=1)
    up_all = jnp.concatenate([up_weight, swapped[1]], axis=1)
    down_all = jnp.concatenate([down_weight, swapped[2]], axis=0)
    for first in range(0, planes, group):
        held = got[first : first + group]
        if outs:
            held[0][0] = after(held[0][0], *outs)
        outs.extend(apply(held, gate_all, up_all, down_all))

    order = list(range(1, planes)) + [0]
    sent = {}
    previous = None
    for i, s in enumerate(order):
        mine = outs[s * PLANE : (s + 1) * PLANE]
        back = [mine[0]]
        for j in range(1, PLANE):
            back.append(send(after(mine[j], previous[j]) if previous else mine[j], flip=2 * j))
        sent[s] = previous = back
    handed = hand_pages(kv_pages, page_target, got[-2][1])
    total = None
    for s in order:
        part = jnp.dot(
            blends[s], jnp.concatenate(sent[s], axis=0), preferred_element_type=jnp.float32
        )
        if total is not None:
            part = part + send(total, step=stride).astype(jnp.float32)
        total = part.astype(jnp.bfloat16)
    return (total, handed)


def solution(mesh):
    placed = (
        P(("groups", "expert"), None),
        P(("groups", "expert"), None),
        P(("groups", "expert"), None),
        P(None, "expert"),
        P(None, "expert"),
        P("expert", None),
        P(("groups", "expert"), None, None),
        P(("groups", "expert")),
    )
    return jax.shard_map(
        local,
        mesh=mesh,
        in_specs=placed,
        out_specs=(P(("groups", "expert"), None), P(("groups", "expert"), None, None)),
        check_vma=False,
    )
```

```python
import functools

import jax
import jax.numpy as jnp
from jax import lax
from jax.experimental import pallas as pl
from jax.experimental.pallas import tpu as pltpu
from jax.sharding import PartitionSpec as P

PCAP = 1
PLANE = 4


def slot_ranks(labels, count):
    onehot = (labels[:, None] == jnp.arange(count, dtype=jnp.int32)[None, :]).astype(jnp.int32)
    earlier = jnp.cumsum(onehot, axis=0) - onehot
    return jnp.sum(earlier * onehot, axis=1)


def place_pages(arrived, arrived_labels, page_count, page_shape):
    picking = (
        arrived_labels.astype(jnp.float32)[None, :]
        == jnp.arange(page_count, dtype=jnp.float32)[:, None]
    ).astype(jnp.bfloat16)
    landed = jnp.dot(picking, arrived, preferred_element_type=jnp.float32)
    return landed.astype(jnp.bfloat16).reshape(page_shape)


def hand_pages(kv_pages, page_target, earlier):
    page_count = kv_pages.shape[0]
    owners = lax.axis_size("expert")
    target_dev = page_target // page_count
    target_slot = page_target % page_count
    flat_pages = kv_pages.reshape(page_count, -1)
    position = target_dev * PCAP + slot_ranks(target_dev, owners)
    placing = position[:, None] == jnp.arange(owners * PCAP, dtype=jnp.int32)[None, :]
    outgoing = lax.dot_general(
        placing.astype(jnp.bfloat16),
        flat_pages,
        (((0,), (0,)), ((), ())),
        preferred_element_type=jnp.float32,
    ).astype(jnp.bfloat16)
    labels = jnp.sum(jnp.where(placing, target_slot[:, None] + 1, 0), axis=0) - 1
    arrived, arrived_labels = (
        lax.all_to_all(after(outgoing, earlier), "expert", split_axis=0, concat_axis=0, tiled=True),
        lax.all_to_all(
            labels.astype(jnp.bfloat16), "expert", split_axis=0, concat_axis=0, tiled=True
        ),
    )
    return place_pages(arrived, arrived_labels, page_count, kv_pages.shape)


def send(x, step=None, flip=None):
    count = lax.axis_size("expert")
    if flip is not None:
        pairs = [(i, i ^ flip) for i in range(count)]
    else:
        pairs = [(i, (i + step) % count) for i in range(count)]
    return lax.ppermute(x, "expert", pairs)


def after(x, *earlier):
    return lax.optimization_barrier((x, *earlier))[0]


def mixing_table(route_ids, route_gates, experts):
    shares = route_gates / jnp.sum(route_gates, axis=1, keepdims=True)
    mixing = shares.astype(jnp.bfloat16).astype(jnp.float32)
    hits = route_ids[:, :, None] == jnp.arange(experts, dtype=jnp.int32)
    return jnp.sum(jnp.where(hits, mixing[:, :, None], 0.0), axis=1).astype(jnp.bfloat16)


def spread(experts, capacity, chip):
    lane = lax.broadcasted_iota(jnp.int32, (experts, PLANE * capacity), 1)
    near = sum((lane >= capacity * j).astype(jnp.int32) for j in range(1, PLANE))
    near = (chip // PLANE) * PLANE + ((chip % PLANE) ^ near)
    expert = lax.broadcasted_iota(jnp.int32, (experts, PLANE * capacity), 0)
    return (expert == near).astype(jnp.float32).astype(jnp.bfloat16)


def slots_of(table, capacity, chip):
    rows, experts = table.shape
    weight = jnp.dot(table, spread(experts, capacity, chip), preferred_element_type=jnp.float32)
    named = weight > 0
    row = lax.broadcasted_iota(jnp.int32, (rows, rows), 0)
    below = (row > lax.broadcasted_iota(jnp.int32, (rows, rows), 1)).astype(jnp.float32)
    rank = jnp.dot(
        below.astype(jnp.bfloat16),
        named.astype(jnp.float32).astype(jnp.bfloat16),
        preferred_element_type=jnp.float32,
    )
    lane = lax.broadcasted_iota(jnp.int32, (rows, PLANE * capacity), 1)
    slot = lane - capacity * sum((lane >= capacity * j).astype(jnp.int32) for j in range(1, PLANE))
    hits = (rank == slot.astype(jnp.float32)) & named
    placing = jnp.where(hits, 1.0, 0.0).astype(jnp.bfloat16)
    blend = jnp.where(hits, weight, 0.0).astype(jnp.bfloat16)
    return placing, blend


def pick(placing, rows):
    return lax.dot_general(
        placing, rows, (((0,), (0,)), ((), ())), preferred_element_type=jnp.float32
    )


def pick_kernel(experts, capacity, step, chip_ref, block_ref, *outs):
    width = outs[0].shape[1]
    blend_ref = outs[PLANE]
    placing, blend = slots_of(block_ref[:, width : width + experts], capacity, chip_ref[0])
    blend_ref[...] = blend
    for at in range(0, width, step):
        found = pick(placing, block_ref[:, at : at + step])
        for j in range(PLANE):
            outs[j][:, at : at + step] = found[capacity * j : capacity * (j + 1)].astype(
                jnp.bfloat16
            )


def first_kernel(experts, capacity, step, chip_ref, tokens_ref, ids_ref, gates_ref, *outs):
    rows, width = tokens_ref.shape
    block_ref = outs[PLANE + 1]
    gates = gates_ref[...]
    shares = gates / jnp.sum(gates, axis=1, keepdims=True)
    mixing = shares.astype(jnp.bfloat16).astype(jnp.float32)
    lane = lax.broadcasted_iota(jnp.int32, (rows, block_ref.shape[1] - width), 1)
    table = jnp.zeros(lane.shape, jnp.float32)
    for k in range(gates.shape[1]):
        table = table + jnp.where(ids_ref[:, k : k + 1] == lane, mixing[:, k : k + 1], 0.0)
    block_ref[:, width:] = table.astype(jnp.bfloat16)
    block_ref[:, :width] = tokens_ref[...]
    pick_kernel(experts, capacity, step, chip_ref, block_ref, *outs[: PLANE + 1])


def pick_pieces(chip, block, width, experts, capacity, routing=None):
    rows = block.shape[0]
    piece = jax.ShapeDtypeStruct((capacity, width), jnp.bfloat16)
    outs = [piece] * PLANE + [jax.ShapeDtypeStruct((rows, PLANE * capacity), jnp.bfloat16)]
    if routing:
        lanes = experts + -experts % 128
        outs.append(jax.ShapeDtypeStruct((rows, width + lanes), jnp.bfloat16))
    body = first_kernel if routing else pick_kernel
    operands = (block, *routing) if routing else (block,)
    return pl.pallas_call(
        functools.partial(body, experts, capacity, 512),
        out_shape=outs,
        in_specs=[pl.BlockSpec(memory_space=pltpu.SMEM)]
        + [pl.BlockSpec(memory_space=pltpu.VMEM)] * len(operands),
        out_specs=[pl.BlockSpec(memory_space=pltpu.VMEM)] * len(outs),
        compiler_params=pltpu.CompilerParams(vmem_limit_bytes=16 * 2**20),
        cost_estimate=pl.CostEstimate(
            flops=2 * rows * PLANE * capacity * width,
            bytes_accessed=2 * width * (rows + PLANE * capacity),
            transcendentals=0,
        ),
    )(jnp.reshape(chip, (1,)), *operands)


def expert_kernel(pieces, steps, *refs):
    rows_in, weights = refs[:pieces], refs[pieces : pieces + 6]
    outs, hidden = refs[pieces + 6 : 2 * pieces + 6], refs[2 * pieces + 6]
    sums = refs[2 * pieces + 7 :]
    i = pl.program_id(0)
    half = hidden.shape[1] // 2

    @pl.when(i == 0)
    def _():
        for total in sums:
            total[...] = jnp.zeros_like(total)

    @pl.when(i < steps)
    def _():
        rows = jnp.concatenate([ref[...].astype(jnp.float32) for ref in rows_in], axis=0)
        rows = rows.astype(jnp.bfloat16)
        for total, weight in zip(sums, weights[:4]):
            total[...] += jnp.dot(rows, weight[...], preferred_element_type=jnp.float32)

    @pl.when(i == steps - 1)
    def _():
        for n in range(2):
            gate = sums[n][...]
            value = gate / (1.0 + jnp.exp(-gate)) * sums[2 + n][...]
            hidden[:, n * half : (n + 1) * half] = value.astype(jnp.bfloat16)

    @pl.when(i >= steps)
    def _():
        down = jnp.concatenate([weights[4][...], weights[5][...]], axis=0)
        out = jnp.dot(hidden[...], down, preferred_element_type=jnp.float32)
        each = out.shape[0] // pieces
        for n in range(pieces):
            outs[n][...] = out[n * each : (n + 1) * each].astype(jnp.bfloat16)


def apply(held, gate, up, down):
    pieces = [piece for arrived in held for piece in arrived]
    each, width = pieces[0].shape
    rows, half = each * len(pieces), gate[0].shape[1]
    step = 1024
    steps = width // step
    read = lambda i: jnp.minimum(i, steps - 1)
    write = lambda i: jnp.maximum(i - steps, 0)
    piece_in = pl.BlockSpec((each, step), lambda i: (0, read(i)))
    piece_out = pl.BlockSpec((each, step), lambda i: (0, write(i)))
    wide = pl.BlockSpec((step, half), lambda i: (read(i), 0))
    tall = pl.BlockSpec((half, step), lambda i: (0, write(i)))
    return pl.pallas_call(
        functools.partial(expert_kernel, len(pieces), steps),
        grid=(2 * steps,),
        out_shape=[jax.ShapeDtypeStruct((each, width), jnp.bfloat16)] * len(pieces),
        in_specs=[piece_in] * len(pieces) + [wide] * 4 + [tall] * 2,
        out_specs=[piece_out] * len(pieces),
        scratch_shapes=[pltpu.VMEM((rows, 2 * half), jnp.bfloat16)]
        + [pltpu.VMEM((rows, half), jnp.float32)] * 4,
        compiler_params=pltpu.CompilerParams(
            dimension_semantics=("arbitrary",), vmem_limit_bytes=60 * 2**20
        ),
        cost_estimate=pl.CostEstimate(
            flops=12 * rows * width * half,
            bytes_accessed=12 * width * half + 4 * rows * width,
            transcendentals=2 * rows * half,
        ),
    )(*pieces, *gate, *up, *down)


def apply_plain(held, gate, up, down):
    pieces = [piece for arrived in held for piece in arrived]
    rows = jnp.concatenate(pieces, axis=0)
    total = 0.0
    for n in range(2):
        left = jnp.dot(rows, gate[n], preferred_element_type=jnp.float32)
        right = jnp.dot(rows, up[n], preferred_element_type=jnp.float32)
        hidden = (jax.nn.silu(left) * right).astype(jnp.bfloat16)
        total = total + jnp.dot(hidden, down[n], preferred_element_type=jnp.float32)
    return jnp.split(total.astype(jnp.bfloat16), len(pieces), axis=0)


def pick_plain(chip, block, width, experts, capacity, routing=None):
    if routing:
        lanes = jnp.pad(mixing_table(*routing, experts), ((0, 0), (0, -experts % 128)))
        block = jnp.concatenate([block, lanes], axis=1)
    placing, blend = slots_of(block[:, width : width + experts], capacity, chip)
    found = pick(placing, block[:, :width]).astype(jnp.bfloat16)
    outs = jnp.split(found, PLANE, axis=0) + [blend]
    return outs + [block] if routing else outs


def local(
    tokens, route_ids, route_gates, gate_weight, up_weight, down_weight, kv_pages, page_target
):
    tok_rows, width = tokens.shape
    chosen = route_ids.shape[1]
    owners = lax.axis_size("expert")
    experts = owners // 2
    planes = experts // PLANE
    stride = 2 * PLANE
    capacity = min(tok_rows, 5 * tok_rows * chosen // (4 * experts))
    chip = lax.axis_index("expert") // 2
    whole = capacity % 8 == 0 and width % 1024 == 0
    choose, work = (pick_pieces, apply) if whole else (pick_plain, apply_plain)
    weights = (gate_weight, up_weight, down_weight)
    group = 2
    swapped, blends, got, outs = [], [], [], []
    block = tokens
    for s in range(planes):
        if s:
            *pieces, blend = choose(chip, block, width, experts, capacity)
        else:
            *pieces, blend, block = choose(
                chip, tokens, width, experts, capacity, (route_ids, route_gates)
            )
        blends.append(blend)
        if s < 3:
            earlier = [block] + (got[s - 1][1:] if s else [])
            swapped.append(send(after(weights[s], *swapped, *earlier), flip=1))
        for j in range(1, PLANE):
            piece = after(pieces[j], got[s - 1][j]) if s else pieces[j]
            pieces[j] = send(piece, flip=2 * j)
        got.append(pieces)
        if s + 1 < planes:
            block = send(block, step=stride)

    pairs = [(own, other) for own, other in zip(weights, swapped)]
    for first in range(0, planes, group):
        held = got[first : first + group]
        if outs:
            held[0][0] = after(held[0][0], *outs)
        outs.extend(work(held, *pairs))

    order = list(range(1, planes)) + [0]
    sent = {}
    previous = None
    for i, s in enumerate(order):
        mine = outs[s * PLANE : (s + 1) * PLANE]
        back = [mine[0]]
        for j in range(1, PLANE):
            back.append(send(after(mine[j], previous[j]) if previous else mine[j], flip=2 * j))
        sent[s] = previous = back
    handed = hand_pages(kv_pages, page_target, got[-2][1])
    total = None
    for s in order:
        part = jnp.dot(
            blends[s], jnp.concatenate(sent[s], axis=0), preferred_element_type=jnp.float32
        )
        if total is not None:
            part = part + send(total, step=stride).astype(jnp.float32)
        total = part.astype(jnp.bfloat16)
    return (total, handed)


def solution(mesh):
    placed = (
        P(("groups", "expert"), None),
        P(("groups", "expert"), None),
        P(("groups", "expert"), None),
        P(None, "expert"),
        P(None, "expert"),
        P("expert", None),
        P(("groups", "expert"), None, None),
        P(("groups", "expert")),
    )
    return jax.shard_map(
        local,
        mesh=mesh,
        in_specs=placed,
        out_specs=(P(("groups", "expert"), None), P(("groups", "expert"), None, None)),
        check_vma=False,
    )
```

```python
import functools

import jax
import jax.numpy as jnp
from jax import lax
from jax.experimental import pallas as pl
from jax.experimental.pallas import tpu as pltpu
from jax.sharding import PartitionSpec as P

PCAP = 1
PLANE = 4


def slot_ranks(labels, count):
    onehot = (labels[:, None] == jnp.arange(count, dtype=jnp.int32)[None, :]).astype(jnp.int32)
    earlier = jnp.cumsum(onehot, axis=0) - onehot
    return jnp.sum(earlier * onehot, axis=1)


def place_pages(arrived, page_count, page_shape):
    picking = (
        arrived[:, -1].astype(jnp.float32)[None, :]
        == jnp.arange(page_count, dtype=jnp.float32)[:, None]
    ).astype(jnp.bfloat16)
    landed = jnp.dot(picking, arrived[:, :-128], preferred_element_type=jnp.float32)
    return landed.astype(jnp.bfloat16).reshape(page_shape)


def sort_pages(kv_pages, page_target):
    page_count = kv_pages.shape[0]
    owners = lax.axis_size("expert")
    target_dev = page_target // page_count
    target_slot = page_target % page_count
    flat_pages = kv_pages.reshape(page_count, -1)
    position = target_dev * PCAP + slot_ranks(target_dev, owners)
    placing = position[:, None] == jnp.arange(owners * PCAP, dtype=jnp.int32)[None, :]
    outgoing = lax.dot_general(
        placing.astype(jnp.bfloat16),
        flat_pages,
        (((0,), (0,)), ((), ())),
        preferred_element_type=jnp.float32,
    ).astype(jnp.bfloat16)
    labels = jnp.sum(jnp.where(placing, target_slot[:, None] + 1, 0), axis=0) - 1
    labels = jnp.broadcast_to(labels.astype(jnp.bfloat16)[:, None], (owners * PCAP, 128))
    return jnp.concatenate([outgoing, labels], axis=1)


def exchange(x):
    return lax.all_to_all(x, "expert", split_axis=0, concat_axis=0, tiled=True)


def send(x, step=None, flip=None):
    count = lax.axis_size("expert")
    if flip is not None:
        pairs = [(i, i ^ flip) for i in range(count)]
    else:
        pairs = [(i, (i + step) % count) for i in range(count)]
    return lax.ppermute(x, "expert", pairs)


def after(x, *earlier):
    return lax.optimization_barrier((x, *earlier))[0]


def mixing_table(route_ids, route_gates, experts):
    shares = route_gates / jnp.sum(route_gates, axis=1, keepdims=True)
    mixing = shares.astype(jnp.bfloat16).astype(jnp.float32)
    hits = route_ids[:, :, None] == jnp.arange(experts, dtype=jnp.int32)
    return jnp.sum(jnp.where(hits, mixing[:, :, None], 0.0), axis=1).astype(jnp.bfloat16)


def spread(experts, capacity, chip):
    lane = lax.broadcasted_iota(jnp.int32, (experts, PLANE * capacity), 1)
    near = sum((lane >= capacity * j).astype(jnp.int32) for j in range(1, PLANE))
    near = (chip // PLANE) * PLANE + ((chip % PLANE) ^ near)
    expert = lax.broadcasted_iota(jnp.int32, (experts, PLANE * capacity), 0)
    return (expert == near).astype(jnp.float32).astype(jnp.bfloat16)


def slots_of(table, capacity, chip):
    rows, experts = table.shape
    weight = jnp.dot(table, spread(experts, capacity, chip), preferred_element_type=jnp.float32)
    named = weight > 0
    row = lax.broadcasted_iota(jnp.int32, (rows, rows), 0)
    below = (row > lax.broadcasted_iota(jnp.int32, (rows, rows), 1)).astype(jnp.float32)
    rank = jnp.dot(
        below.astype(jnp.bfloat16),
        named.astype(jnp.float32).astype(jnp.bfloat16),
        preferred_element_type=jnp.float32,
    )
    lane = lax.broadcasted_iota(jnp.int32, (rows, PLANE * capacity), 1)
    slot = lane - capacity * sum((lane >= capacity * j).astype(jnp.int32) for j in range(1, PLANE))
    hits = (rank == slot.astype(jnp.float32)) & named
    placing = jnp.where(hits, 1.0, 0.0).astype(jnp.bfloat16)
    blend = jnp.where(hits, weight, 0.0).astype(jnp.bfloat16)
    return placing, blend


def pick(placing, rows):
    return lax.dot_general(
        placing, rows, (((0,), (0,)), ((), ())), preferred_element_type=jnp.float32
    )


def pick_kernel(experts, capacity, step, chip_ref, block_ref, *outs):
    width = outs[0].shape[1]
    blend_ref = outs[PLANE]
    placing, blend = slots_of(block_ref[:, width : width + experts], capacity, chip_ref[0])
    blend_ref[...] = blend
    for at in range(0, width, step):
        found = pick(placing, block_ref[:, at : at + step])
        for j in range(PLANE):
            outs[j][:, at : at + step] = found[capacity * j : capacity * (j + 1)].astype(
                jnp.bfloat16
            )


def first_kernel(experts, capacity, step, chip_ref, tokens_ref, ids_ref, gates_ref, *outs):
    rows, width = tokens_ref.shape
    block_ref = outs[PLANE + 1]
    gates = gates_ref[...]
    shares = gates / jnp.sum(gates, axis=1, keepdims=True)
    mixing = shares.astype(jnp.bfloat16).astype(jnp.float32)
    lane = lax.broadcasted_iota(jnp.int32, (rows, block_ref.shape[1] - width), 1)
    table = jnp.zeros(lane.shape, jnp.float32)
    for k in range(gates.shape[1]):
        table = table + jnp.where(ids_ref[:, k : k + 1] == lane, mixing[:, k : k + 1], 0.0)
    block_ref[:, width:] = table.astype(jnp.bfloat16)
    block_ref[:, :width] = tokens_ref[...]
    pick_kernel(experts, capacity, step, chip_ref, block_ref, *outs[: PLANE + 1])


def pick_pieces(chip, block, width, experts, capacity, routing=None):
    rows = block.shape[0]
    piece = jax.ShapeDtypeStruct((capacity, width), jnp.bfloat16)
    outs = [piece] * PLANE + [jax.ShapeDtypeStruct((rows, PLANE * capacity), jnp.bfloat16)]
    if routing:
        lanes = experts + -experts % 128
        outs.append(jax.ShapeDtypeStruct((rows, width + lanes), jnp.bfloat16))
    body = first_kernel if routing else pick_kernel
    operands = (block, *routing) if routing else (block,)
    return pl.pallas_call(
        functools.partial(body, experts, capacity, 512),
        out_shape=outs,
        in_specs=[pl.BlockSpec(memory_space=pltpu.SMEM)]
        + [pl.BlockSpec(memory_space=pltpu.VMEM)] * len(operands),
        out_specs=[pl.BlockSpec(memory_space=pltpu.VMEM)] * len(outs),
        compiler_params=pltpu.CompilerParams(vmem_limit_bytes=16 * 2**20),
        cost_estimate=pl.CostEstimate(
            flops=2 * rows * PLANE * capacity * width,
            bytes_accessed=2 * width * (rows + PLANE * capacity),
            transcendentals=0,
        ),
    )(jnp.reshape(chip, (1,)), *operands)


def expert_kernel(pieces, steps, *refs):
    rows_in, weights = refs[:pieces], refs[pieces : pieces + 6]
    outs, hidden = refs[pieces + 6 : 2 * pieces + 6], refs[2 * pieces + 6]
    sums = refs[2 * pieces + 7 :]
    i = pl.program_id(0)
    half = hidden.shape[1] // 2

    @pl.when(i == 0)
    def _():
        for total in sums:
            total[...] = jnp.zeros_like(total)

    @pl.when(i < steps)
    def _():
        rows = jnp.concatenate([ref[...].astype(jnp.float32) for ref in rows_in], axis=0)
        rows = rows.astype(jnp.bfloat16)
        for total, weight in zip(sums, weights[:4]):
            total[...] += jnp.dot(rows, weight[...], preferred_element_type=jnp.float32)

    @pl.when(i == steps - 1)
    def _():
        for n in range(2):
            gate = sums[n][...]
            value = gate / (1.0 + jnp.exp(-gate)) * sums[2 + n][...]
            hidden[:, n * half : (n + 1) * half] = value.astype(jnp.bfloat16)

    @pl.when(i >= steps)
    def _():
        down = jnp.concatenate([weights[4][...], weights[5][...]], axis=0)
        out = jnp.dot(hidden[...], down, preferred_element_type=jnp.float32)
        each = out.shape[0] // pieces
        for n in range(pieces):
            outs[n][...] = out[n * each : (n + 1) * each].astype(jnp.bfloat16)


def apply(held, gate, up, down):
    pieces = [piece for arrived in held for piece in arrived]
    each, width = pieces[0].shape
    rows, half = each * len(pieces), gate[0].shape[1]
    step = 1024
    steps = width // step
    read = lambda i: jnp.minimum(i, steps - 1)
    write = lambda i: jnp.maximum(i - steps, 0)
    piece_in = pl.BlockSpec((each, step), lambda i: (0, read(i)))
    piece_out = pl.BlockSpec((each, step), lambda i: (0, write(i)))
    wide = pl.BlockSpec((step, half), lambda i: (read(i), 0))
    tall = pl.BlockSpec((half, step), lambda i: (0, write(i)))
    return pl.pallas_call(
        functools.partial(expert_kernel, len(pieces), steps),
        grid=(2 * steps,),
        out_shape=[jax.ShapeDtypeStruct((each, width), jnp.bfloat16)] * len(pieces),
        in_specs=[piece_in] * len(pieces) + [wide] * 4 + [tall] * 2,
        out_specs=[piece_out] * len(pieces),
        scratch_shapes=[pltpu.VMEM((rows, 2 * half), jnp.bfloat16)]
        + [pltpu.VMEM((rows, half), jnp.float32)] * 4,
        compiler_params=pltpu.CompilerParams(
            dimension_semantics=("arbitrary",), vmem_limit_bytes=60 * 2**20
        ),
        cost_estimate=pl.CostEstimate(
            flops=12 * rows * width * half,
            bytes_accessed=12 * width * half + 4 * rows * width,
            transcendentals=2 * rows * half,
        ),
    )(*pieces, *gate, *up, *down)


def apply_plain(held, gate, up, down):
    pieces = [piece for arrived in held for piece in arrived]
    rows = jnp.concatenate(pieces, axis=0)
    total = 0.0
    for n in range(2):
        left = jnp.dot(rows, gate[n], preferred_element_type=jnp.float32)
        right = jnp.dot(rows, up[n], preferred_element_type=jnp.float32)
        hidden = (jax.nn.silu(left) * right).astype(jnp.bfloat16)
        total = total + jnp.dot(hidden, down[n], preferred_element_type=jnp.float32)
    return jnp.split(total.astype(jnp.bfloat16), len(pieces), axis=0)


def pick_plain(chip, block, width, experts, capacity, routing=None):
    if routing:
        lanes = jnp.pad(mixing_table(*routing, experts), ((0, 0), (0, -experts % 128)))
        block = jnp.concatenate([block, lanes], axis=1)
    placing, blend = slots_of(block[:, width : width + experts], capacity, chip)
    found = pick(placing, block[:, :width]).astype(jnp.bfloat16)
    outs = jnp.split(found, PLANE, axis=0) + [blend]
    return outs + [block] if routing else outs


def local(
    tokens, route_ids, route_gates, gate_weight, up_weight, down_weight, kv_pages, page_target
):
    tok_rows, width = tokens.shape
    chosen = route_ids.shape[1]
    owners = lax.axis_size("expert")
    experts = owners // 2
    planes = experts // PLANE
    stride = 2 * PLANE
    capacity = min(tok_rows, 5 * tok_rows * chosen // (4 * experts))
    chip = lax.axis_index("expert") // 2
    whole = capacity % 8 == 0 and width % 1024 == 0
    choose, work = (pick_pieces, apply) if whole else (pick_plain, apply_plain)
    weights = (gate_weight, up_weight, down_weight)
    group = 2
    swapped, blends, got, outs = [], [], [], []
    outgoing = sort_pages(kv_pages, page_target)
    block = tokens
    for s in range(planes):
        if s:
            *pieces, blend = choose(chip, block, width, experts, capacity)
        else:
            *pieces, blend, block = choose(
                chip, tokens, width, experts, capacity, (route_ids, route_gates)
            )
        blends.append(blend)
        if s < 3:
            earlier = [block] + (got[s - 1][1:] if s else [])
            swapped.append(send(after(weights[s], *swapped, *earlier), flip=1))
        for j in range(1, PLANE):
            piece = after(pieces[j], got[s - 1][j]) if s else pieces[j]
            pieces[j] = send(piece, flip=2 * j)
        got.append(pieces)
        if s + 1 < planes:
            block = send(block, step=stride)

    pairs = [(own, other) for own, other in zip(weights, swapped)]
    for first in range(0, planes, group):
        held = [list(pieces) for pieces in got[first : first + group]]
        following = got[first + group][1:] if first + group < planes else []
        held[0][0] = after(held[0][0], *outs, *following)
        outs.extend(work(held, *pairs))

    arrived = exchange(after(outgoing, *got[-2][1:], block))
    order = list(range(1, planes)) + [0]
    sent, landed = {}, got[-1][1:]
    for s in order:
        mine = outs[s * PLANE : (s + 1) * PLANE]
        sent[s] = [mine[0]]
        for j in range(1, PLANE):
            waits = [landed[-3 if s == 1 else -4]] + ([arrived] if s == order[-2] else [])
            landed.append(send(after(mine[j], *waits), flip=2 * j))
            sent[s].append(landed[-1])
    handed = place_pages(arrived, kv_pages.shape[0], kv_pages.shape)
    sent[1][0] = after(sent[1][0], outs[-1])
    total = None
    for s in order:
        part = jnp.dot(
            blends[s], jnp.concatenate(sent[s], axis=0), preferred_element_type=jnp.float32
        )
        if total is not None:
            part = part + send(total, step=stride).astype(jnp.float32)
        total = part.astype(jnp.bfloat16)
    return (total, handed)


def solution(mesh):
    placed = (
        P(("groups", "expert"), None),
        P(("groups", "expert"), None),
        P(("groups", "expert"), None),
        P(None, "expert"),
        P(None, "expert"),
        P("expert", None),
        P(("groups", "expert"), None, None),
        P(("groups", "expert")),
    )
    return jax.shard_map(
        local,
        mesh=mesh,
        in_specs=placed,
        out_specs=(P(("groups", "expert"), None), P(("groups", "expert"), None, None)),
        check_vma=False,
    )
```

```python
import functools

import jax
import jax.numpy as jnp
from jax import lax
from jax.experimental import pallas as pl
from jax.experimental.pallas import tpu as pltpu
from jax.sharding import PartitionSpec as P

PCAP = 1
PLANE = 4


LANES = 128


def sort_kernel(target_ref, pages_ref, out_ref):
    count, rows, width = pages_ref.shape
    if out_ref.shape[0] > count:
        out_ref[...] = jnp.full(out_ref.shape, -1.0, out_ref.dtype)

    @pl.loop(0, count)
    def _(p):
        target = target_ref[p]
        owner = target // count
        slot = (target - owner * count).astype(jnp.float32)
        out_ref[owner, :, :width] = pages_ref[p]
        out_ref[owner, :, width:] = jnp.full((rows, LANES), slot, jnp.float32).astype(jnp.bfloat16)


def sort_pages(kv_pages, page_target):
    count, rows, width = kv_pages.shape
    owners = lax.axis_size("expert")
    return pl.pallas_call(
        sort_kernel,
        out_shape=jax.ShapeDtypeStruct((owners * PCAP, rows, width + LANES), jnp.bfloat16),
        in_specs=[
            pl.BlockSpec(memory_space=pltpu.SMEM),
            pl.BlockSpec(memory_space=pltpu.VMEM),
        ],
        out_specs=pl.BlockSpec(memory_space=pltpu.VMEM),
        compiler_params=pltpu.CompilerParams(vmem_limit_bytes=16 * 2**20),
        cost_estimate=pl.CostEstimate(
            flops=0, bytes_accessed=6 * count * rows * width, transcendentals=0
        ),
    )(page_target, kv_pages)


def place_kernel(label_ref, arrived_ref, out_ref):
    sources = arrived_ref.shape[0]
    width = out_ref.shape[2]

    @pl.loop(0, sources)
    def _(p):
        label = label_ref[p]

        @pl.when((label >= 0) & (label < out_ref.shape[0]))
        def _():
            out_ref[label] = arrived_ref[p, :, :width]


def place_pages(arrived, page_shape):
    count, rows, width = page_shape
    labels = arrived[:, 0, width].astype(jnp.int32)
    return pl.pallas_call(
        place_kernel,
        out_shape=jax.ShapeDtypeStruct(page_shape, jnp.bfloat16),
        in_specs=[
            pl.BlockSpec(memory_space=pltpu.SMEM),
            pl.BlockSpec(memory_space=pltpu.VMEM),
        ],
        out_specs=pl.BlockSpec(memory_space=pltpu.VMEM),
        compiler_params=pltpu.CompilerParams(vmem_limit_bytes=16 * 2**20),
        cost_estimate=pl.CostEstimate(
            flops=0, bytes_accessed=4 * count * rows * width, transcendentals=0
        ),
    )(labels, arrived)


def exchange(x):
    return lax.all_to_all(x, "expert", split_axis=0, concat_axis=0, tiled=True)


def send(x, step=None, flip=None):
    count = lax.axis_size("expert")
    if flip is not None:
        pairs = [(i, i ^ flip) for i in range(count)]
    else:
        pairs = [(i, (i + step) % count) for i in range(count)]
    return lax.ppermute(x, "expert", pairs)


def after(x, *earlier):
    return lax.optimization_barrier((x, *earlier))[0]


def mixing_table(route_ids, route_gates, experts):
    shares = route_gates / jnp.sum(route_gates, axis=1, keepdims=True)
    mixing = shares.astype(jnp.bfloat16).astype(jnp.float32)
    hits = route_ids[:, :, None] == jnp.arange(experts, dtype=jnp.int32)
    return jnp.sum(jnp.where(hits, mixing[:, :, None], 0.0), axis=1).astype(jnp.bfloat16)


def spread(experts, capacity, chip):
    lane = lax.broadcasted_iota(jnp.int32, (experts, PLANE * capacity), 1)
    near = sum((lane >= capacity * j).astype(jnp.int32) for j in range(1, PLANE))
    near = (chip // PLANE) * PLANE + ((chip % PLANE) ^ near)
    expert = lax.broadcasted_iota(jnp.int32, (experts, PLANE * capacity), 0)
    return (expert == near).astype(jnp.float32).astype(jnp.bfloat16)


def slots_of(table, capacity, chip):
    rows, experts = table.shape
    weight = jnp.dot(table, spread(experts, capacity, chip), preferred_element_type=jnp.float32)
    named = weight > 0
    row = lax.broadcasted_iota(jnp.int32, (rows, rows), 0)
    below = (row > lax.broadcasted_iota(jnp.int32, (rows, rows), 1)).astype(jnp.float32)
    rank = jnp.dot(
        below.astype(jnp.bfloat16),
        named.astype(jnp.float32).astype(jnp.bfloat16),
        preferred_element_type=jnp.float32,
    )
    lane = lax.broadcasted_iota(jnp.int32, (rows, PLANE * capacity), 1)
    slot = lane - capacity * sum((lane >= capacity * j).astype(jnp.int32) for j in range(1, PLANE))
    hits = (rank == slot.astype(jnp.float32)) & named
    placing = jnp.where(hits, 1.0, 0.0).astype(jnp.bfloat16)
    blend = jnp.where(hits, weight, 0.0).astype(jnp.bfloat16)
    return placing, blend


def pick(placing, rows):
    return lax.dot_general(
        placing, rows, (((0,), (0,)), ((), ())), preferred_element_type=jnp.float32
    )


def pick_kernel(experts, capacity, step, chip_ref, block_ref, *outs):
    width = outs[0].shape[1]
    blend_ref = outs[PLANE]
    placing, blend = slots_of(block_ref[:, width : width + experts], capacity, chip_ref[0])
    blend_ref[...] = blend
    for at in range(0, width, step):
        found = pick(placing, block_ref[:, at : at + step])
        for j in range(PLANE):
            outs[j][:, at : at + step] = found[capacity * j : capacity * (j + 1)].astype(
                jnp.bfloat16
            )


def first_kernel(experts, capacity, step, chip_ref, tokens_ref, ids_ref, gates_ref, *outs):
    rows, width = tokens_ref.shape
    block_ref = outs[PLANE + 1]
    gates = gates_ref[...]
    shares = gates / jnp.sum(gates, axis=1, keepdims=True)
    mixing = shares.astype(jnp.bfloat16).astype(jnp.float32)
    lane = lax.broadcasted_iota(jnp.int32, (rows, block_ref.shape[1] - width), 1)
    table = jnp.zeros(lane.shape, jnp.float32)
    for k in range(gates.shape[1]):
        table = table + jnp.where(ids_ref[:, k : k + 1] == lane, mixing[:, k : k + 1], 0.0)
    block_ref[:, width:] = table.astype(jnp.bfloat16)
    block_ref[:, :width] = tokens_ref[...]
    pick_kernel(experts, capacity, step, chip_ref, block_ref, *outs[: PLANE + 1])


def pick_pieces(chip, block, width, experts, capacity, routing=None):
    rows = block.shape[0]
    piece = jax.ShapeDtypeStruct((capacity, width), jnp.bfloat16)
    outs = [piece] * PLANE + [jax.ShapeDtypeStruct((rows, PLANE * capacity), jnp.bfloat16)]
    if routing:
        lanes = experts + -experts % 128
        outs.append(jax.ShapeDtypeStruct((rows, width + lanes), jnp.bfloat16))
    body = first_kernel if routing else pick_kernel
    operands = (block, *routing) if routing else (block,)
    return pl.pallas_call(
        functools.partial(body, experts, capacity, 512),
        out_shape=outs,
        in_specs=[pl.BlockSpec(memory_space=pltpu.SMEM)]
        + [pl.BlockSpec(memory_space=pltpu.VMEM)] * len(operands),
        out_specs=[pl.BlockSpec(memory_space=pltpu.VMEM)] * len(outs),
        compiler_params=pltpu.CompilerParams(vmem_limit_bytes=16 * 2**20),
        cost_estimate=pl.CostEstimate(
            flops=2 * rows * PLANE * capacity * width,
            bytes_accessed=2 * width * (rows + PLANE * capacity),
            transcendentals=0,
        ),
    )(jnp.reshape(chip, (1,)), *operands)


def expert_kernel(pieces, steps, *refs):
    rows_in, weights = refs[:pieces], refs[pieces : pieces + 6]
    outs, hidden = refs[pieces + 6 : 2 * pieces + 6], refs[2 * pieces + 6]
    sums = refs[2 * pieces + 7 :]
    i = pl.program_id(0)
    half = hidden.shape[1] // 2

    @pl.when(i == 0)
    def _():
        for total in sums:
            total[...] = jnp.zeros_like(total)

    @pl.when(i < steps)
    def _():
        rows = jnp.concatenate([ref[...].astype(jnp.float32) for ref in rows_in], axis=0)
        rows = rows.astype(jnp.bfloat16)
        for total, weight in zip(sums, weights[:4]):
            total[...] += jnp.dot(rows, weight[...], preferred_element_type=jnp.float32)

    @pl.when(i == steps - 1)
    def _():
        for n in range(2):
            gate = sums[n][...]
            value = gate / (1.0 + jnp.exp(-gate)) * sums[2 + n][...]
            hidden[:, n * half : (n + 1) * half] = value.astype(jnp.bfloat16)

    @pl.when(i >= steps)
    def _():
        down = jnp.concatenate([weights[4][...], weights[5][...]], axis=0)
        out = jnp.dot(hidden[...], down, preferred_element_type=jnp.float32)
        each = out.shape[0] // pieces
        for n in range(pieces):
            outs[n][...] = out[n * each : (n + 1) * each].astype(jnp.bfloat16)


def apply(held, gate, up, down):
    pieces = [piece for arrived in held for piece in arrived]
    each, width = pieces[0].shape
    rows, half = each * len(pieces), gate[0].shape[1]
    step = 1024
    steps = width // step
    read = lambda i: jnp.minimum(i, steps - 1)
    write = lambda i: jnp.maximum(i - steps, 0)
    piece_in = pl.BlockSpec((each, step), lambda i: (0, read(i)))
    piece_out = pl.BlockSpec((each, step), lambda i: (0, write(i)))
    wide = pl.BlockSpec((step, half), lambda i: (read(i), 0))
    tall = pl.BlockSpec((half, step), lambda i: (0, write(i)))
    return pl.pallas_call(
        functools.partial(expert_kernel, len(pieces), steps),
        grid=(2 * steps,),
        out_shape=[jax.ShapeDtypeStruct((each, width), jnp.bfloat16)] * len(pieces),
        in_specs=[piece_in] * len(pieces) + [wide] * 4 + [tall] * 2,
        out_specs=[piece_out] * len(pieces),
        scratch_shapes=[pltpu.VMEM((rows, 2 * half), jnp.bfloat16)]
        + [pltpu.VMEM((rows, half), jnp.float32)] * 4,
        compiler_params=pltpu.CompilerParams(
            dimension_semantics=("arbitrary",), vmem_limit_bytes=60 * 2**20
        ),
        cost_estimate=pl.CostEstimate(
            flops=12 * rows * width * half,
            bytes_accessed=12 * width * half + 4 * rows * width,
            transcendentals=2 * rows * half,
        ),
    )(*pieces, *gate, *up, *down)


def apply_plain(held, gate, up, down):
    pieces = [piece for arrived in held for piece in arrived]
    rows = jnp.concatenate(pieces, axis=0)
    total = 0.0
    for n in range(2):
        left = jnp.dot(rows, gate[n], preferred_element_type=jnp.float32)
        right = jnp.dot(rows, up[n], preferred_element_type=jnp.float32)
        hidden = (jax.nn.silu(left) * right).astype(jnp.bfloat16)
        total = total + jnp.dot(hidden, down[n], preferred_element_type=jnp.float32)
    return jnp.split(total.astype(jnp.bfloat16), len(pieces), axis=0)


def pick_plain(chip, block, width, experts, capacity, routing=None):
    if routing:
        lanes = jnp.pad(mixing_table(*routing, experts), ((0, 0), (0, -experts % 128)))
        block = jnp.concatenate([block, lanes], axis=1)
    placing, blend = slots_of(block[:, width : width + experts], capacity, chip)
    found = pick(placing, block[:, :width]).astype(jnp.bfloat16)
    outs = jnp.split(found, PLANE, axis=0) + [blend]
    return outs + [block] if routing else outs


def local(
    tokens, route_ids, route_gates, gate_weight, up_weight, down_weight, kv_pages, page_target
):
    tok_rows, width = tokens.shape
    chosen = route_ids.shape[1]
    owners = lax.axis_size("expert")
    experts = owners // 2
    planes = experts // PLANE
    stride = 2 * PLANE
    capacity = min(tok_rows, 5 * tok_rows * chosen // (4 * experts))
    chip = lax.axis_index("expert") // 2
    whole = capacity % 8 == 0 and width % 1024 == 0
    choose, work = (pick_pieces, apply) if whole else (pick_plain, apply_plain)
    weights = (gate_weight, up_weight, down_weight)
    group = 2
    swapped, blends, got, outs = [], [], [], []
    outgoing = sort_pages(kv_pages, page_target)
    block = tokens
    for s in range(planes):
        if s:
            *pieces, blend = choose(chip, block, width, experts, capacity)
        else:
            *pieces, blend, block = choose(
                chip, tokens, width, experts, capacity, (route_ids, route_gates)
            )
        blends.append(blend)
        if s < 3:
            earlier = [block] + (got[s - 1][1:] if s else [])
            swapped.append(send(after(weights[s], *swapped, *earlier), flip=1))
        for j in range(1, PLANE):
            piece = after(pieces[j], got[s - 1][j]) if s else pieces[j]
            pieces[j] = send(piece, flip=2 * j)
        got.append(pieces)
        if s + 1 < planes:
            block = send(block, step=stride)

    for first in range(0, planes, group):
        held = [list(pieces) for pieces in got[first : first + group]]
        following = got[first + group][1:] if first + group < planes else []
        held[0][0] = after(held[0][0], *outs, *following)
        outs.extend(work(held, *zip(weights, swapped)))

    arrived = exchange(after(outgoing, outs[0]))
    order = list(range(1, planes)) + [0]
    sent, landed = {}, got[-1][1:]
    for s in order:
        mine = outs[s * PLANE : (s + 1) * PLANE]
        sent[s] = [mine[0]]
        for j in range(1, PLANE):
            waits = [landed[-3 if s == 1 else -4]] + ([arrived] if s == 0 else [])
            landed.append(send(after(mine[j], *waits), flip=2 * j))
            sent[s].append(landed[-1])
    handed = place_pages(arrived, kv_pages.shape)
    sent[1][0] = after(sent[1][0], outs[-1])
    total = None
    for s in order:
        part = jnp.dot(
            blends[s], jnp.concatenate(sent[s], axis=0), preferred_element_type=jnp.float32
        )
        if total is not None:
            part = part + send(total, step=stride).astype(jnp.float32)
        total = part.astype(jnp.bfloat16)
    return (total, handed)


def solution(mesh):
    placed = (
        P(("groups", "expert"), None),
        P(("groups", "expert"), None),
        P(("groups", "expert"), None),
        P(None, "expert"),
        P(None, "expert"),
        P("expert", None),
        P(("groups", "expert"), None, None),
        P(("groups", "expert")),
    )
    return jax.shard_map(
        local,
        mesh=mesh,
        in_specs=placed,
        out_specs=(P(("groups", "expert"), None), P(("groups", "expert"), None, None)),
        check_vma=False,
    )
```

```python
import functools

import jax
import jax.numpy as jnp
from jax import lax
from jax.experimental import pallas as pl
from jax.experimental.pallas import tpu as pltpu
from jax.sharding import PartitionSpec as P

PCAP = 1
PLANE = 4


LANES = 128


def sort_kernel(target_ref, pages_ref, out_ref):
    count, rows, width = pages_ref.shape
    if out_ref.shape[0] > count:
        out_ref[...] = jnp.full(out_ref.shape, -1.0, out_ref.dtype)

    @pl.loop(0, count)
    def _(p):
        target = target_ref[p]
        owner = target // count
        slot = (target - owner * count).astype(jnp.float32)
        out_ref[owner, :, :width] = pages_ref[p]
        out_ref[owner, :, width:] = jnp.full((rows, LANES), slot, jnp.float32).astype(jnp.bfloat16)


def sort_pages(kv_pages, page_target):
    count, rows, width = kv_pages.shape
    owners = lax.axis_size("expert")
    return pl.pallas_call(
        sort_kernel,
        out_shape=jax.ShapeDtypeStruct((owners * PCAP, rows, width + LANES), jnp.bfloat16),
        in_specs=[
            pl.BlockSpec(memory_space=pltpu.SMEM),
            pl.BlockSpec(memory_space=pltpu.VMEM),
        ],
        out_specs=pl.BlockSpec(memory_space=pltpu.VMEM),
        compiler_params=pltpu.CompilerParams(vmem_limit_bytes=16 * 2**20),
        cost_estimate=pl.CostEstimate(
            flops=0, bytes_accessed=6 * count * rows * width, transcendentals=0
        ),
    )(page_target, kv_pages)


def place_kernel(label_ref, arrived_ref, out_ref):
    sources = arrived_ref.shape[0]
    width = out_ref.shape[2]

    @pl.loop(0, sources)
    def _(p):
        label = label_ref[p]

        @pl.when((label >= 0) & (label < out_ref.shape[0]))
        def _():
            out_ref[label] = arrived_ref[p, :, :width]


def place_pages(arrived, page_shape):
    count, rows, width = page_shape
    labels = arrived[:, 0, width].astype(jnp.int32)
    return pl.pallas_call(
        place_kernel,
        out_shape=jax.ShapeDtypeStruct(page_shape, jnp.bfloat16),
        in_specs=[
            pl.BlockSpec(memory_space=pltpu.SMEM),
            pl.BlockSpec(memory_space=pltpu.VMEM),
        ],
        out_specs=pl.BlockSpec(memory_space=pltpu.VMEM),
        compiler_params=pltpu.CompilerParams(vmem_limit_bytes=16 * 2**20),
        cost_estimate=pl.CostEstimate(
            flops=0, bytes_accessed=4 * count * rows * width, transcendentals=0
        ),
    )(labels, arrived)


def exchange(x):
    return lax.all_to_all(x, "expert", split_axis=0, concat_axis=0, tiled=True)


def send(x, step=None, flip=None):
    count = lax.axis_size("expert")
    if flip is not None:
        pairs = [(i, i ^ flip) for i in range(count)]
    else:
        pairs = [(i, (i + step) % count) for i in range(count)]
    return lax.ppermute(x, "expert", pairs)


def after(x, *earlier):
    return lax.optimization_barrier((x, *earlier))[0]


def mixing_table(route_ids, route_gates, experts):
    shares = route_gates / jnp.sum(route_gates, axis=1, keepdims=True)
    mixing = shares.astype(jnp.bfloat16).astype(jnp.float32)
    hits = route_ids[:, :, None] == jnp.arange(experts, dtype=jnp.int32)
    return jnp.sum(jnp.where(hits, mixing[:, :, None], 0.0), axis=1).astype(jnp.bfloat16)


def spread(experts, capacity, chip):
    lane = lax.broadcasted_iota(jnp.int32, (experts, PLANE * capacity), 1)
    near = sum((lane >= capacity * j).astype(jnp.int32) for j in range(1, PLANE))
    near = (chip // PLANE) * PLANE + ((chip % PLANE) ^ near)
    expert = lax.broadcasted_iota(jnp.int32, (experts, PLANE * capacity), 0)
    return (expert == near).astype(jnp.float32).astype(jnp.bfloat16)


def slots_of(table, capacity, chip):
    rows, experts = table.shape
    weight = jnp.dot(table, spread(experts, capacity, chip), preferred_element_type=jnp.float32)
    named = weight > 0
    row = lax.broadcasted_iota(jnp.int32, (rows, rows), 0)
    below = (row > lax.broadcasted_iota(jnp.int32, (rows, rows), 1)).astype(jnp.float32)
    rank = jnp.dot(
        below.astype(jnp.bfloat16),
        named.astype(jnp.float32).astype(jnp.bfloat16),
        preferred_element_type=jnp.float32,
    )
    lane = lax.broadcasted_iota(jnp.int32, (rows, PLANE * capacity), 1)
    slot = lane - capacity * sum((lane >= capacity * j).astype(jnp.int32) for j in range(1, PLANE))
    hits = (rank == slot.astype(jnp.float32)) & named
    placing = jnp.where(hits, 1.0, 0.0).astype(jnp.bfloat16)
    blend = jnp.where(hits, weight, 0.0).astype(jnp.bfloat16)
    return placing, blend


def pick(placing, rows):
    return lax.dot_general(
        placing, rows, (((0,), (0,)), ((), ())), preferred_element_type=jnp.float32
    )


def pick_kernel(experts, capacity, step, chip_ref, block_ref, *outs):
    width = outs[0].shape[1]
    blend_ref = outs[PLANE - 1]
    placing, blend = slots_of(block_ref[:, width : width + experts], capacity, chip_ref[0])
    blend_ref[...] = blend
    for at in range(0, width, step):
        found = pick(placing, block_ref[:, at : at + step])
        for j in range(1, PLANE):
            part = found[capacity * j : capacity * (j + 1)]
            outs[j - 1][:, at : at + step] = part.astype(jnp.bfloat16)


def first_kernel(experts, capacity, step, chip_ref, tokens_ref, ids_ref, gates_ref, *outs):
    rows, width = tokens_ref.shape
    block_ref = outs[PLANE]
    ids = ids_ref[...].astype(jnp.float32).T.astype(jnp.int32)
    gates = gates_ref[...].T
    shares = gates / jnp.sum(gates, axis=1, keepdims=True)
    mixing = shares.astype(jnp.bfloat16).astype(jnp.float32)
    lane = lax.broadcasted_iota(jnp.int32, (rows, block_ref.shape[1] - width), 1)
    table = jnp.zeros(lane.shape, jnp.float32)
    for k in range(gates.shape[1]):
        table = table + jnp.where(ids[:, k : k + 1] == lane, mixing[:, k : k + 1], 0.0)
    block_ref[:, width:] = table.astype(jnp.bfloat16)
    block_ref[:, :width] = tokens_ref[...]
    pick_kernel(experts, capacity, step, chip_ref, block_ref, *outs[:PLANE])


def pick_pieces(chip, block, width, experts, capacity, routing=None):
    rows = block.shape[0]
    piece = jax.ShapeDtypeStruct((capacity, width), jnp.bfloat16)
    outs = [piece] * (PLANE - 1) + [jax.ShapeDtypeStruct((rows, PLANE * capacity), jnp.bfloat16)]
    if routing:
        lanes = experts + -experts % 128
        outs.append(jax.ShapeDtypeStruct((rows, width + lanes), jnp.bfloat16))
    body = first_kernel if routing else pick_kernel
    operands = (block, routing[0].T, routing[1].T) if routing else (block,)
    found = pl.pallas_call(
        functools.partial(body, experts, capacity, 512),
        out_shape=outs,
        in_specs=[pl.BlockSpec(memory_space=pltpu.SMEM)]
        + [pl.BlockSpec(memory_space=pltpu.VMEM)] * len(operands),
        out_specs=[pl.BlockSpec(memory_space=pltpu.VMEM)] * len(outs),
        compiler_params=pltpu.CompilerParams(vmem_limit_bytes=16 * 2**20),
        cost_estimate=pl.CostEstimate(
            flops=2 * rows * PLANE * capacity * width,
            bytes_accessed=2 * width * (rows + PLANE * capacity),
            transcendentals=0,
        ),
    )(jnp.reshape(chip, (1,)), *operands)
    placing = (found[PLANE - 1][:, :capacity] > 0).astype(jnp.bfloat16)
    return [pick(placing, block[:, :width]).astype(jnp.bfloat16), *found]


def expert_kernel(pieces, steps, *refs):
    rows_in, weights = refs[:pieces], refs[pieces : pieces + 6]
    outs, hidden = refs[pieces + 6 : 2 * pieces + 6], refs[2 * pieces + 6]
    sums = refs[2 * pieces + 7 :]
    i = pl.program_id(0)
    half = hidden.shape[1] // 2

    @pl.when(i == 0)
    def _():
        for total in sums:
            total[...] = jnp.zeros_like(total)

    @pl.when(i < steps)
    def _():
        rows = jnp.concatenate([ref[...].astype(jnp.float32) for ref in rows_in], axis=0)
        rows = rows.astype(jnp.bfloat16)
        for total, weight in zip(sums, weights[:4]):
            total[...] += jnp.dot(rows, weight[...], preferred_element_type=jnp.float32)

    @pl.when(i == steps - 1)
    def _():
        for n in range(2):
            gate = sums[n][...]
            value = gate / (1.0 + jnp.exp(-gate)) * sums[2 + n][...]
            hidden[:, n * half : (n + 1) * half] = value.astype(jnp.bfloat16)

    @pl.when(i >= steps)
    def _():
        down = jnp.concatenate([weights[4][...], weights[5][...]], axis=0)
        out = jnp.dot(hidden[...], down, preferred_element_type=jnp.float32)
        each = out.shape[0] // pieces
        for n in range(pieces):
            outs[n][...] = out[n * each : (n + 1) * each].astype(jnp.bfloat16)


def apply(held, gate, up, down):
    pieces = [piece for arrived in held for piece in arrived]
    each, width = pieces[0].shape
    rows, half = each * len(pieces), gate[0].shape[1]
    step = 1024
    steps = width // step
    read = lambda i: jnp.minimum(i, steps - 1)
    write = lambda i: jnp.maximum(i - steps, 0)
    piece_in = pl.BlockSpec((each, step), lambda i: (0, read(i)))
    piece_out = pl.BlockSpec((each, step), lambda i: (0, write(i)))
    wide = pl.BlockSpec((step, half), lambda i: (read(i), 0))
    tall = pl.BlockSpec((half, step), lambda i: (0, write(i)))
    return pl.pallas_call(
        functools.partial(expert_kernel, len(pieces), steps),
        grid=(2 * steps,),
        out_shape=[jax.ShapeDtypeStruct((each, width), jnp.bfloat16)] * len(pieces),
        in_specs=[piece_in] * len(pieces) + [wide] * 4 + [tall] * 2,
        out_specs=[piece_out] * len(pieces),
        scratch_shapes=[pltpu.VMEM((rows, 2 * half), jnp.bfloat16)]
        + [pltpu.VMEM((rows, half), jnp.float32)] * 4,
        compiler_params=pltpu.CompilerParams(
            dimension_semantics=("arbitrary",), vmem_limit_bytes=60 * 2**20
        ),
        cost_estimate=pl.CostEstimate(
            flops=12 * rows * width * half,
            bytes_accessed=12 * width * half + 4 * rows * width,
            transcendentals=2 * rows * half,
        ),
    )(*pieces, *gate, *up, *down)


def apply_plain(held, gate, up, down):
    pieces = [piece for arrived in held for piece in arrived]
    rows = jnp.concatenate(pieces, axis=0)
    total = 0.0
    for n in range(2):
        left = jnp.dot(rows, gate[n], preferred_element_type=jnp.float32)
        right = jnp.dot(rows, up[n], preferred_element_type=jnp.float32)
        hidden = (jax.nn.silu(left) * right).astype(jnp.bfloat16)
        total = total + jnp.dot(hidden, down[n], preferred_element_type=jnp.float32)
    return jnp.split(total.astype(jnp.bfloat16), len(pieces), axis=0)


def pick_plain(chip, block, width, experts, capacity, routing=None):
    if routing:
        lanes = jnp.pad(mixing_table(*routing, experts), ((0, 0), (0, -experts % 128)))
        block = jnp.concatenate([block, lanes], axis=1)
    placing, blend = slots_of(block[:, width : width + experts], capacity, chip)
    found = pick(placing, block[:, :width]).astype(jnp.bfloat16)
    outs = jnp.split(found, PLANE, axis=0) + [blend]
    return outs + [block] if routing else outs


def local(
    tokens, route_ids, route_gates, gate_weight, up_weight, down_weight, kv_pages, page_target
):
    tok_rows, width = tokens.shape
    chosen = route_ids.shape[1]
    owners = lax.axis_size("expert")
    experts = owners // 2
    planes = experts // PLANE
    stride = 2 * PLANE
    capacity = min(tok_rows, 5 * tok_rows * chosen // (4 * experts))
    chip = lax.axis_index("expert") // 2
    whole = capacity % 8 == 0 and width % 1024 == 0
    choose, work = (pick_pieces, apply) if whole else (pick_plain, apply_plain)
    weights = (gate_weight, up_weight, down_weight)
    group = 2
    swapped, blends, got, outs = [], [], [], []
    outgoing = sort_pages(kv_pages, page_target)
    block = tokens
    for s in range(planes):
        if s:
            *pieces, blend = choose(chip, block, width, experts, capacity)
        else:
            *pieces, blend, block = choose(
                chip, tokens, width, experts, capacity, (route_ids, route_gates)
            )
        blends.append(blend)
        if s < 3:
            earlier = [block] + (got[s - 1][1:] if s else []) + ([outgoing] if s == 1 else [])
            swapped.append(send(after(weights[s], *swapped, *earlier), flip=1))
        for j in range(1, PLANE):
            piece = after(pieces[j], got[s - 1][j]) if s else pieces[j]
            pieces[j] = send(piece, flip=2 * j)
        got.append(pieces)
        if s + 1 < planes:
            block = send(block, step=stride)

    for first in range(0, planes, group):
        held = [list(pieces) for pieces in got[first : first + group]]
        following = got[first + group][1:] if first + group < planes else []
        held[0][0] = after(held[0][0], *outs, *following)
        outs.extend(work(held, *zip(weights, swapped)))

    arrived = exchange(after(outgoing, *got[-2][1:], block))
    order = list(range(1, planes)) + [0]
    sent, landed = {}, got[-1][1:]
    for s in order:
        mine = outs[s * PLANE : (s + 1) * PLANE]
        sent[s] = [mine[0]]
        for j in range(1, PLANE):
            waits = [landed[-3 if s == 1 else -4]] + ([arrived] if s == 0 else [])
            landed.append(send(after(mine[j], *waits), flip=2 * j))
            sent[s].append(landed[-1])
    handed = place_pages(arrived, kv_pages.shape)
    sent[1][0] = after(sent[1][0], outs[-1])
    total = None
    for s in order:
        part = jnp.dot(
            blends[s], jnp.concatenate(sent[s], axis=0), preferred_element_type=jnp.float32
        )
        if total is not None:
            part = part + send(total, step=stride).astype(jnp.float32)
        total = part.astype(jnp.bfloat16)
    return (total, handed)


def solution(mesh):
    placed = (
        P(("groups", "expert"), None),
        P(("groups", "expert"), None),
        P(("groups", "expert"), None),
        P(None, "expert"),
        P(None, "expert"),
        P("expert", None),
        P(("groups", "expert"), None, None),
        P(("groups", "expert")),
    )
    return jax.shard_map(
        local,
        mesh=mesh,
        in_specs=placed,
        out_specs=(P(("groups", "expert"), None), P(("groups", "expert"), None, None)),
        check_vma=False,
    )
```

```python
import functools

import jax
import jax.numpy as jnp
from jax import lax
from jax.experimental import pallas as pl
from jax.experimental.pallas import tpu as pltpu
from jax.sharding import PartitionSpec as P

PCAP = 1
PLANE = 4


LANES = 128


def sort_kernel(target_ref, pages_ref, out_ref):
    count, rows, width = pages_ref.shape
    if out_ref.shape[0] > count:
        out_ref[...] = jnp.full(out_ref.shape, -1.0, out_ref.dtype)

    @pl.loop(0, count)
    def _(p):
        target = target_ref[p]
        owner = target // count
        slot = (target - owner * count).astype(jnp.float32)
        out_ref[owner, :, :width] = pages_ref[p]
        out_ref[owner, :, width:] = jnp.full((rows, LANES), slot, jnp.float32).astype(jnp.bfloat16)


def sort_pages(kv_pages, page_target):
    count, rows, width = kv_pages.shape
    owners = lax.axis_size("expert")
    return pl.pallas_call(
        sort_kernel,
        out_shape=jax.ShapeDtypeStruct((owners * PCAP, rows, width + LANES), jnp.bfloat16),
        in_specs=[
            pl.BlockSpec(memory_space=pltpu.SMEM),
            pl.BlockSpec(memory_space=pltpu.VMEM),
        ],
        out_specs=pl.BlockSpec(memory_space=pltpu.VMEM),
        compiler_params=pltpu.CompilerParams(vmem_limit_bytes=16 * 2**20),
        cost_estimate=pl.CostEstimate(
            flops=0, bytes_accessed=6 * count * rows * width, transcendentals=0
        ),
    )(page_target, kv_pages)


def place_kernel(label_ref, arrived_ref, out_ref):
    sources = arrived_ref.shape[0]
    width = out_ref.shape[2]

    @pl.loop(0, sources)
    def _(p):
        label = label_ref[p]

        @pl.when((label >= 0) & (label < out_ref.shape[0]))
        def _():
            out_ref[label] = arrived_ref[p, :, :width]


def place_pages(arrived, page_shape):
    count, rows, width = page_shape
    labels = arrived[:, 0, width].astype(jnp.int32)
    return pl.pallas_call(
        place_kernel,
        out_shape=jax.ShapeDtypeStruct(page_shape, jnp.bfloat16),
        in_specs=[
            pl.BlockSpec(memory_space=pltpu.SMEM),
            pl.BlockSpec(memory_space=pltpu.VMEM),
        ],
        out_specs=pl.BlockSpec(memory_space=pltpu.VMEM),
        compiler_params=pltpu.CompilerParams(vmem_limit_bytes=16 * 2**20),
        cost_estimate=pl.CostEstimate(
            flops=0, bytes_accessed=4 * count * rows * width, transcendentals=0
        ),
    )(labels, arrived)


def exchange(x):
    return lax.all_to_all(x, "expert", split_axis=0, concat_axis=0, tiled=True)


def send(x, step=None, flip=None):
    count = lax.axis_size("expert")
    if flip is not None:
        pairs = [(i, i ^ flip) for i in range(count)]
    else:
        pairs = [(i, (i + step) % count) for i in range(count)]
    return lax.ppermute(x, "expert", pairs)


def after(x, *earlier):
    return lax.optimization_barrier((x, *earlier))[0]


def gather(weight, dimension):
    pairs = [[i, i + 1] for i in range(0, lax.axis_size("expert"), 2)]
    return lax.all_gather(weight, "expert", axis=dimension, tiled=True, axis_index_groups=pairs)


def mixing_table(route_ids, route_gates, experts):
    shares = route_gates / jnp.sum(route_gates, axis=1, keepdims=True)
    mixing = shares.astype(jnp.bfloat16).astype(jnp.float32)
    hits = route_ids[:, :, None] == jnp.arange(experts, dtype=jnp.int32)
    return jnp.sum(jnp.where(hits, mixing[:, :, None], 0.0), axis=1).astype(jnp.bfloat16)


def spread(experts, capacity, chip):
    lane = lax.broadcasted_iota(jnp.int32, (experts, PLANE * capacity), 1)
    near = sum((lane >= capacity * j).astype(jnp.int32) for j in range(1, PLANE))
    near = (chip // PLANE) * PLANE + ((chip % PLANE) ^ near)
    expert = lax.broadcasted_iota(jnp.int32, (experts, PLANE * capacity), 0)
    return (expert == near).astype(jnp.float32).astype(jnp.bfloat16)


def slots_of(table, capacity, chip):
    rows, experts = table.shape
    weight = jnp.dot(table, spread(experts, capacity, chip), preferred_element_type=jnp.float32)
    named = weight > 0
    row = lax.broadcasted_iota(jnp.int32, (rows, rows), 0)
    below = (row > lax.broadcasted_iota(jnp.int32, (rows, rows), 1)).astype(jnp.float32)
    rank = jnp.dot(
        below.astype(jnp.bfloat16),
        named.astype(jnp.float32).astype(jnp.bfloat16),
        preferred_element_type=jnp.float32,
    )
    lane = lax.broadcasted_iota(jnp.int32, (rows, PLANE * capacity), 1)
    slot = lane - capacity * sum((lane >= capacity * j).astype(jnp.int32) for j in range(1, PLANE))
    hits = (rank == slot.astype(jnp.float32)) & named
    placing = jnp.where(hits, 1.0, 0.0).astype(jnp.bfloat16)
    blend = jnp.where(hits, weight, 0.0).astype(jnp.bfloat16)
    return placing, blend


def pick(placing, rows):
    return lax.dot_general(
        placing, rows, (((0,), (0,)), ((), ())), preferred_element_type=jnp.float32
    )


def pick_kernel(experts, capacity, step, chip_ref, block_ref, *outs):
    width = outs[0].shape[1]
    blend_ref = outs[PLANE - 1]
    placing, blend = slots_of(block_ref[:, width : width + experts], capacity, chip_ref[0])
    blend_ref[...] = blend
    for at in range(0, width, step):
        found = pick(placing, block_ref[:, at : at + step])
        for j in range(1, PLANE):
            part = found[capacity * j : capacity * (j + 1)]
            outs[j - 1][:, at : at + step] = part.astype(jnp.bfloat16)


def first_kernel(experts, capacity, step, chip_ref, tokens_ref, ids_ref, gates_ref, *outs):
    rows, width = tokens_ref.shape
    block_ref = outs[PLANE]
    ids = ids_ref[...].astype(jnp.float32).T.astype(jnp.int32)
    gates = gates_ref[...].T
    shares = gates / jnp.sum(gates, axis=1, keepdims=True)
    mixing = shares.astype(jnp.bfloat16).astype(jnp.float32)
    lane = lax.broadcasted_iota(jnp.int32, (rows, block_ref.shape[1] - width), 1)
    table = jnp.zeros(lane.shape, jnp.float32)
    for k in range(gates.shape[1]):
        table = table + jnp.where(ids[:, k : k + 1] == lane, mixing[:, k : k + 1], 0.0)
    block_ref[:, width:] = table.astype(jnp.bfloat16)
    block_ref[:, :width] = tokens_ref[...]
    pick_kernel(experts, capacity, step, chip_ref, block_ref, *outs[:PLANE])


def pick_pieces(chip, block, width, experts, capacity, routing=None):
    rows = block.shape[0]
    piece = jax.ShapeDtypeStruct((capacity, width), jnp.bfloat16)
    outs = [piece] * (PLANE - 1) + [jax.ShapeDtypeStruct((rows, PLANE * capacity), jnp.bfloat16)]
    if routing:
        lanes = experts + -experts % 128
        outs.append(jax.ShapeDtypeStruct((rows, width + lanes), jnp.bfloat16))
    body = first_kernel if routing else pick_kernel
    operands = (block, routing[0].T, routing[1].T) if routing else (block,)
    found = pl.pallas_call(
        functools.partial(body, experts, capacity, 512),
        out_shape=outs,
        in_specs=[pl.BlockSpec(memory_space=pltpu.SMEM)]
        + [pl.BlockSpec(memory_space=pltpu.VMEM)] * len(operands),
        out_specs=[pl.BlockSpec(memory_space=pltpu.VMEM)] * len(outs),
        compiler_params=pltpu.CompilerParams(vmem_limit_bytes=16 * 2**20),
        cost_estimate=pl.CostEstimate(
            flops=200 * rows * PLANE * capacity * width,
            bytes_accessed=2 * width * (rows + PLANE * capacity),
            transcendentals=0,
        ),
    )(jnp.reshape(chip, (1,)), *operands)
    placing = (found[PLANE - 1][:, :capacity] > 0).astype(jnp.bfloat16)
    return [pick(placing, block[:, :width]).astype(jnp.bfloat16), *found]


def expert_kernel(pieces, steps, *refs):
    rows_in, (gate_ref, up_ref, down_ref) = refs[:pieces], refs[pieces : pieces + 3]
    outs = refs[pieces + 3 : 2 * pieces + 3]
    rows, hidden = refs[2 * pieces + 3 :]
    i = pl.program_id(0)
    width = rows.shape[1]
    part = gate_ref.shape[1]

    @pl.when(i == 0)
    def _():
        for at in range(0, width, 512):
            found = [ref[:, at : at + 512].astype(jnp.float32) for ref in rows_in]
            rows[:, at : at + 512] = jnp.concatenate(found, axis=0).astype(jnp.bfloat16)

    @pl.when(i < steps)
    def _():
        wide = jnp.concatenate([gate_ref[...], up_ref[...]], axis=1)
        found = jnp.dot(rows[...], wide, preferred_element_type=jnp.float32)
        gate, up = found[:, :part], found[:, part:]
        hidden[i] = (gate / (1.0 + jnp.exp(-gate)) * up).astype(jnp.bfloat16)

    @pl.when(i >= steps)
    def _():
        left = jnp.concatenate([hidden[n] for n in range(steps)], axis=1)
        out = jnp.dot(left, down_ref[...], preferred_element_type=jnp.float32)
        each = out.shape[0] // pieces
        for n in range(pieces):
            outs[n][...] = out[n * each : (n + 1) * each].astype(jnp.bfloat16)


def apply(held, gate, up, down):
    pieces = [piece for arrived in held for piece in arrived]
    each, width = pieces[0].shape
    rows, units = each * len(pieces), gate.shape[1]
    part, span = 256, 1024
    steps = units // part
    read = lambda i: jnp.minimum(i, steps - 1)
    write = lambda i: jnp.maximum(i - steps, 0)
    piece_in = pl.BlockSpec((each, width), lambda i: (0, 0))
    piece_out = pl.BlockSpec((each, span), lambda i: (0, write(i)))
    wide = pl.BlockSpec((width, part), lambda i: (0, read(i)))
    tall = pl.BlockSpec((units, span), lambda i: (0, write(i)))
    return pl.pallas_call(
        functools.partial(expert_kernel, len(pieces), steps),
        grid=(steps + width // span,),
        out_shape=[jax.ShapeDtypeStruct((each, width), jnp.bfloat16)] * len(pieces),
        in_specs=[piece_in] * len(pieces) + [wide] * 2 + [tall],
        out_specs=[piece_out] * len(pieces),
        scratch_shapes=[
            pltpu.VMEM((rows, width), jnp.bfloat16),
            pltpu.VMEM((steps, rows, part), jnp.bfloat16),
        ],
        compiler_params=pltpu.CompilerParams(
            dimension_semantics=("arbitrary",), vmem_limit_bytes=60 * 2**20
        ),
        cost_estimate=pl.CostEstimate(
            flops=6 * rows * width * units,
            bytes_accessed=6 * width * units + 4 * rows * width,
            transcendentals=rows * units,
        ),
    )(*pieces, gate, up, down)


def apply_plain(held, gate_weight, up_weight, down_weight):
    pieces = [piece for arrived in held for piece in arrived]
    rows = jnp.concatenate(pieces, axis=0)
    gate = jnp.dot(rows, gate_weight, preferred_element_type=jnp.float32)
    up = jnp.dot(rows, up_weight, preferred_element_type=jnp.float32)
    hidden = (jax.nn.silu(gate) * up).astype(jnp.bfloat16)
    out = jnp.dot(hidden, down_weight, preferred_element_type=jnp.float32)
    return jnp.split(out.astype(jnp.bfloat16), len(pieces), axis=0)


def pick_plain(chip, block, width, experts, capacity, routing=None):
    if routing:
        lanes = jnp.pad(mixing_table(*routing, experts), ((0, 0), (0, -experts % 128)))
        block = jnp.concatenate([block, lanes], axis=1)
    placing, blend = slots_of(block[:, width : width + experts], capacity, chip)
    found = pick(placing, block[:, :width]).astype(jnp.bfloat16)
    outs = jnp.split(found, PLANE, axis=0) + [blend]
    return outs + [block] if routing else outs


def local(
    tokens, route_ids, route_gates, gate_weight, up_weight, down_weight, kv_pages, page_target
):
    tok_rows, width = tokens.shape
    chosen = route_ids.shape[1]
    owners = lax.axis_size("expert")
    experts = owners // 2
    planes = experts // PLANE
    stride = 2 * PLANE
    capacity = min(tok_rows, 5 * tok_rows * chosen // (4 * experts))
    chip = lax.axis_index("expert") // 2
    whole = capacity % 8 == 0 and width % 1024 == 0
    choose, work = (pick_pieces, apply) if whole else (pick_plain, apply_plain)
    weights = [gather(gate_weight, 1), gather(up_weight, 1), gather(down_weight, 0)]
    group = 2
    blends, got, outs = [], [], []
    outgoing = sort_pages(kv_pages, page_target)
    block = tokens
    for s in range(planes):
        if s:
            *pieces, blend = choose(chip, block, width, experts, capacity)
        else:
            *pieces, blend, block = choose(
                chip, tokens, width, experts, capacity, (route_ids, route_gates)
            )
        blends.append(blend)
        for j in range(1, PLANE):
            piece = after(pieces[j], got[s - 1][j]) if s else pieces[j]
            pieces[j] = send(piece, flip=2 * j)
        got.append(pieces)
        if s + 1 < planes:
            block = send(block, step=stride)

    for first in range(0, planes, group):
        held = [list(pieces) for pieces in got[first : first + group]]
        following = got[first + group][1:] if first + group < planes else []
        held[0][0] = after(held[0][0], *outs, *following)
        outs.extend(work(held, *weights))

    arrived = exchange(after(outgoing, block))
    order = list(range(1, planes)) + [0]
    sent, landed = {}, got[-1][1:]
    for s in order:
        mine = outs[s * PLANE : (s + 1) * PLANE]
        sent[s] = [mine[0]]
        for j in range(1, PLANE):
            waits = [landed[-3 if s == 1 else -4]] + ([arrived] if s == 0 else [])
            landed.append(send(after(mine[j], *waits), flip=2 * j))
            sent[s].append(landed[-1])
    handed = place_pages(arrived, kv_pages.shape)
    sent[1][0] = after(sent[1][0], outs[-1])
    total = None
    for s in order:
        part = jnp.dot(
            blends[s], jnp.concatenate(sent[s], axis=0), preferred_element_type=jnp.float32
        )
        if total is not None:
            part = part + send(total, step=stride).astype(jnp.float32)
        total = part.astype(jnp.bfloat16)
    return (total, handed)


def solution(mesh):
    placed = (
        P(("groups", "expert"), None),
        P(("groups", "expert"), None),
        P(("groups", "expert"), None),
        P(None, "expert"),
        P(None, "expert"),
        P("expert", None),
        P(("groups", "expert"), None, None),
        P(("groups", "expert")),
    )
    return jax.shard_map(
        local,
        mesh=mesh,
        in_specs=placed,
        out_specs=(P(("groups", "expert"), None), P(("groups", "expert"), None, None)),
        check_vma=False,
    )
```

```python
import functools

import jax
import jax.numpy as jnp
from jax import lax
from jax.experimental import pallas as pl
from jax.experimental.pallas import tpu as pltpu
from jax.sharding import PartitionSpec as P

PCAP = 1
PLANE = 4


LANES = 128


def sort_kernel(target_ref, pages_ref, out_ref):
    count, rows, width = pages_ref.shape
    if out_ref.shape[0] > count:
        out_ref[...] = jnp.full(out_ref.shape, -1.0, out_ref.dtype)

    @pl.loop(0, count)
    def _(p):
        target = target_ref[p]
        owner = target // count
        slot = (target - owner * count).astype(jnp.float32)
        out_ref[owner, :, :width] = pages_ref[p]
        out_ref[owner, :, width:] = jnp.full((rows, LANES), slot, jnp.float32).astype(jnp.bfloat16)


def sort_pages(kv_pages, page_target):
    count, rows, width = kv_pages.shape
    owners = lax.axis_size("expert")
    return pl.pallas_call(
        sort_kernel,
        out_shape=jax.ShapeDtypeStruct((owners * PCAP, rows, width + LANES), jnp.bfloat16),
        in_specs=[
            pl.BlockSpec(memory_space=pltpu.SMEM),
            pl.BlockSpec(memory_space=pltpu.VMEM),
        ],
        out_specs=pl.BlockSpec(memory_space=pltpu.VMEM),
        compiler_params=pltpu.CompilerParams(vmem_limit_bytes=16 * 2**20),
        cost_estimate=pl.CostEstimate(
            flops=0, bytes_accessed=6 * count * rows * width, transcendentals=0
        ),
    )(page_target, kv_pages)


def place_kernel(label_ref, arrived_ref, out_ref):
    sources = arrived_ref.shape[0]
    width = out_ref.shape[2]

    @pl.loop(0, sources)
    def _(p):
        label = label_ref[p]

        @pl.when((label >= 0) & (label < out_ref.shape[0]))
        def _():
            out_ref[label] = arrived_ref[p, :, :width]


def place_pages(arrived, page_shape):
    count, rows, width = page_shape
    labels = arrived[:, 0, width].astype(jnp.int32)
    return pl.pallas_call(
        place_kernel,
        out_shape=jax.ShapeDtypeStruct(page_shape, jnp.bfloat16),
        in_specs=[
            pl.BlockSpec(memory_space=pltpu.SMEM),
            pl.BlockSpec(memory_space=pltpu.VMEM),
        ],
        out_specs=pl.BlockSpec(memory_space=pltpu.VMEM),
        compiler_params=pltpu.CompilerParams(vmem_limit_bytes=16 * 2**20),
        cost_estimate=pl.CostEstimate(
            flops=0, bytes_accessed=4 * count * rows * width, transcendentals=0
        ),
    )(labels, arrived)


def exchange(x):
    return lax.all_to_all(x, "expert", split_axis=0, concat_axis=0, tiled=True)


def send(x, step=None, flip=None):
    count = lax.axis_size("expert")
    if flip is not None:
        pairs = [(i, i ^ flip) for i in range(count)]
    else:
        pairs = [(i, (i + step) % count) for i in range(count)]
    return lax.ppermute(x, "expert", pairs)


def after(x, *earlier):
    return lax.optimization_barrier((x, *earlier))[0]


def mixing_table(route_ids, route_gates, experts):
    shares = route_gates / jnp.sum(route_gates, axis=1, keepdims=True)
    mixing = shares.astype(jnp.bfloat16).astype(jnp.float32)
    hits = route_ids[:, :, None] == jnp.arange(experts, dtype=jnp.int32)
    return jnp.sum(jnp.where(hits, mixing[:, :, None], 0.0), axis=1).astype(jnp.bfloat16)


def spread(experts, capacity, chip):
    lane = lax.broadcasted_iota(jnp.int32, (experts, PLANE * capacity), 1)
    near = sum((lane >= capacity * j).astype(jnp.int32) for j in range(1, PLANE))
    near = (chip // PLANE) * PLANE + ((chip % PLANE) ^ near)
    expert = lax.broadcasted_iota(jnp.int32, (experts, PLANE * capacity), 0)
    return (expert == near).astype(jnp.float32).astype(jnp.bfloat16)


def slots_of(table, capacity, chip):
    rows, experts = table.shape
    weight = jnp.dot(table, spread(experts, capacity, chip), preferred_element_type=jnp.float32)
    named = weight > 0
    row = lax.broadcasted_iota(jnp.int32, (rows, rows), 0)
    below = (row > lax.broadcasted_iota(jnp.int32, (rows, rows), 1)).astype(jnp.float32)
    rank = jnp.dot(
        below.astype(jnp.bfloat16),
        named.astype(jnp.float32).astype(jnp.bfloat16),
        preferred_element_type=jnp.float32,
    )
    lane = lax.broadcasted_iota(jnp.int32, (rows, PLANE * capacity), 1)
    slot = lane - capacity * sum((lane >= capacity * j).astype(jnp.int32) for j in range(1, PLANE))
    hits = (rank == slot.astype(jnp.float32)) & named
    placing = jnp.where(hits, 1.0, 0.0).astype(jnp.bfloat16)
    blend = jnp.where(hits, weight, 0.0).astype(jnp.bfloat16)
    return placing, blend


def pick(placing, rows):
    return lax.dot_general(
        placing, rows, (((0,), (0,)), ((), ())), preferred_element_type=jnp.float32
    )


def pick_kernel(experts, capacity, step, chip_ref, block_ref, *outs):
    width = outs[0].shape[1]
    blend_ref = outs[PLANE - 1]
    placing, blend = slots_of(block_ref[:, width : width + experts], capacity, chip_ref[0])
    blend_ref[...] = blend
    for at in range(0, width, step):
        found = pick(placing, block_ref[:, at : at + step])
        for j in range(1, PLANE):
            part = found[capacity * j : capacity * (j + 1)]
            outs[j - 1][:, at : at + step] = part.astype(jnp.bfloat16)


def first_kernel(experts, capacity, step, chip_ref, tokens_ref, ids_ref, gates_ref, *outs):
    rows, width = tokens_ref.shape
    block_ref = outs[PLANE]
    ids = ids_ref[...].astype(jnp.float32).T.astype(jnp.int32)
    gates = gates_ref[...].T
    shares = gates / jnp.sum(gates, axis=1, keepdims=True)
    mixing = shares.astype(jnp.bfloat16).astype(jnp.float32)
    lane = lax.broadcasted_iota(jnp.int32, (rows, block_ref.shape[1] - width), 1)
    table = jnp.zeros(lane.shape, jnp.float32)
    for k in range(gates.shape[1]):
        table = table + jnp.where(ids[:, k : k + 1] == lane, mixing[:, k : k + 1], 0.0)
    block_ref[:, width:] = table.astype(jnp.bfloat16)
    block_ref[:, :width] = tokens_ref[...]
    pick_kernel(experts, capacity, step, chip_ref, block_ref, *outs[:PLANE])


def pick_pieces(chip, block, width, experts, capacity, routing=None):
    rows = block.shape[0]
    piece = jax.ShapeDtypeStruct((capacity, width), jnp.bfloat16)
    outs = [piece] * (PLANE - 1) + [jax.ShapeDtypeStruct((rows, PLANE * capacity), jnp.bfloat16)]
    if routing:
        lanes = experts + -experts % 128
        outs.append(jax.ShapeDtypeStruct((rows, width + lanes), jnp.bfloat16))
    body = first_kernel if routing else pick_kernel
    operands = (block, routing[0].T, routing[1].T) if routing else (block,)
    found = pl.pallas_call(
        functools.partial(body, experts, capacity, 512),
        out_shape=outs,
        in_specs=[pl.BlockSpec(memory_space=pltpu.SMEM)]
        + [pl.BlockSpec(memory_space=pltpu.VMEM)] * len(operands),
        out_specs=[pl.BlockSpec(memory_space=pltpu.VMEM)] * len(outs),
        compiler_params=pltpu.CompilerParams(vmem_limit_bytes=16 * 2**20),
        cost_estimate=pl.CostEstimate(
            flops=1200 * rows * PLANE * capacity * width,
            bytes_accessed=2 * width * (rows + PLANE * capacity),
            transcendentals=0,
        ),
    )(jnp.reshape(chip, (1,)), *operands)
    placing = (found[PLANE - 1][:, :capacity] > 0).astype(jnp.bfloat16)
    return [pick(placing, block[:, :width]).astype(jnp.bfloat16), *found]


def expert_kernel(pieces, steps, *refs):
    rows_in, weights = refs[:pieces], refs[pieces : pieces + 6]
    outs, hidden = refs[pieces + 6 : 2 * pieces + 6], refs[2 * pieces + 6]
    sums = refs[2 * pieces + 7 :]
    i = pl.program_id(0)
    half = hidden.shape[1] // 2

    @pl.when(i == 0)
    def _():
        for total in sums:
            total[...] = jnp.zeros_like(total)

    @pl.when(i < steps)
    def _():
        rows = jnp.concatenate([ref[...].astype(jnp.float32) for ref in rows_in], axis=0)
        rows = rows.astype(jnp.bfloat16)
        for total, weight in zip(sums, weights[:4]):
            total[...] += jnp.dot(rows, weight[...], preferred_element_type=jnp.float32)

    @pl.when(i == steps - 1)
    def _():
        for n in range(2):
            gate = sums[n][...]
            value = gate / (1.0 + jnp.exp(-gate)) * sums[2 + n][...]
            hidden[:, n * half : (n + 1) * half] = value.astype(jnp.bfloat16)

    @pl.when(i >= steps)
    def _():
        down = jnp.concatenate([weights[4][...], weights[5][...]], axis=0)
        out = jnp.dot(hidden[...], down, preferred_element_type=jnp.float32)
        each = out.shape[0] // pieces
        for n in range(pieces):
            outs[n][...] = out[n * each : (n + 1) * each].astype(jnp.bfloat16)


def apply(held, gate, up, down):
    pieces = [piece for arrived in held for piece in arrived]
    each, width = pieces[0].shape
    rows, half = each * len(pieces), gate[0].shape[1]
    step = 1024
    steps = width // step
    read = lambda i: jnp.minimum(i, steps - 1)
    write = lambda i: jnp.maximum(i - steps, 0)
    piece_in = pl.BlockSpec((each, step), lambda i: (0, read(i)))
    piece_out = pl.BlockSpec((each, step), lambda i: (0, write(i)))
    wide = pl.BlockSpec((step, half), lambda i: (read(i), 0))
    tall = pl.BlockSpec((half, step), lambda i: (0, write(i)))
    return pl.pallas_call(
        functools.partial(expert_kernel, len(pieces), steps),
        grid=(2 * steps,),
        out_shape=[jax.ShapeDtypeStruct((each, width), jnp.bfloat16)] * len(pieces),
        in_specs=[piece_in] * len(pieces) + [wide] * 4 + [tall] * 2,
        out_specs=[piece_out] * len(pieces),
        scratch_shapes=[pltpu.VMEM((rows, 2 * half), jnp.bfloat16)]
        + [pltpu.VMEM((rows, half), jnp.float32)] * 4,
        compiler_params=pltpu.CompilerParams(
            dimension_semantics=("arbitrary",), vmem_limit_bytes=60 * 2**20
        ),
        cost_estimate=pl.CostEstimate(
            flops=12 * rows * width * half,
            bytes_accessed=12 * width * half + 4 * rows * width,
            transcendentals=2 * rows * half,
        ),
    )(*pieces, *gate, *up, *down)


def apply_plain(held, gate, up, down):
    pieces = [piece for arrived in held for piece in arrived]
    rows = jnp.concatenate(pieces, axis=0)
    total = 0.0
    for n in range(2):
        left = jnp.dot(rows, gate[n], preferred_element_type=jnp.float32)
        right = jnp.dot(rows, up[n], preferred_element_type=jnp.float32)
        hidden = (jax.nn.silu(left) * right).astype(jnp.bfloat16)
        total = total + jnp.dot(hidden, down[n], preferred_element_type=jnp.float32)
    return jnp.split(total.astype(jnp.bfloat16), len(pieces), axis=0)


def pick_plain(chip, block, width, experts, capacity, routing=None):
    if routing:
        lanes = jnp.pad(mixing_table(*routing, experts), ((0, 0), (0, -experts % 128)))
        block = jnp.concatenate([block, lanes], axis=1)
    placing, blend = slots_of(block[:, width : width + experts], capacity, chip)
    found = pick(placing, block[:, :width]).astype(jnp.bfloat16)
    outs = jnp.split(found, PLANE, axis=0) + [blend]
    return outs + [block] if routing else outs


def local(
    tokens, route_ids, route_gates, gate_weight, up_weight, down_weight, kv_pages, page_target
):
    tok_rows, width = tokens.shape
    chosen = route_ids.shape[1]
    owners = lax.axis_size("expert")
    experts = owners // 2
    planes = experts // PLANE
    stride = 2 * PLANE
    capacity = min(tok_rows, 5 * tok_rows * chosen // (4 * experts))
    chip = lax.axis_index("expert") // 2
    whole = capacity % 8 == 0 and width % 1024 == 0
    choose, work = (pick_pieces, apply) if whole else (pick_plain, apply_plain)
    weights = (gate_weight, up_weight, down_weight)
    group = 2
    swapped, blends, got, outs = [], [], [], []
    outgoing = sort_pages(kv_pages, page_target)
    block = tokens
    for s in range(planes):
        if s:
            *pieces, blend = choose(chip, block, width, experts, capacity)
        else:
            *pieces, blend, block = choose(
                chip, tokens, width, experts, capacity, (route_ids, route_gates)
            )
        blends.append(blend)
        if s < 3:
            swapped.append(send(after(weights[s], *swapped, block), flip=1))
        for j in range(1, PLANE):
            piece = after(pieces[j], got[s - 1][j]) if s else pieces[j]
            pieces[j] = send(piece, flip=2 * j)
        got.append(pieces)
        if s + 1 < planes:
            block = send(block, step=stride)

    for first in range(0, planes, group):
        held = [list(pieces) for pieces in got[first : first + group]]
        following = got[first + group][1:] if first + group < planes else []
        held[0][0] = after(held[0][0], *outs, *following)
        outs.extend(work(held, *zip(weights, swapped)))

    arrived = exchange(after(outgoing, block))
    order = list(range(1, planes)) + [0]
    sent, landed = {}, got[-1][1:]
    for s in order:
        mine = outs[s * PLANE : (s + 1) * PLANE]
        sent[s] = [mine[0]]
        for j in range(1, PLANE):
            waits = [landed[-3 if s == 1 else -4]] + ([arrived] if s == 0 else [])
            landed.append(send(after(mine[j], *waits), flip=2 * j))
            sent[s].append(landed[-1])
    handed = place_pages(arrived, kv_pages.shape)
    sent[1][0] = after(sent[1][0], outs[-1])
    total = None
    for s in order:
        part = jnp.dot(
            blends[s], jnp.concatenate(sent[s], axis=0), preferred_element_type=jnp.float32
        )
        if total is not None:
            part = part + send(total, step=stride).astype(jnp.float32)
        total = part.astype(jnp.bfloat16)
    return (total, handed)


def solution(mesh):
    placed = (
        P(("groups", "expert"), None),
        P(("groups", "expert"), None),
        P(("groups", "expert"), None),
        P(None, "expert"),
        P(None, "expert"),
        P("expert", None),
        P(("groups", "expert"), None, None),
        P(("groups", "expert")),
    )
    return jax.shard_map(
        local,
        mesh=mesh,
        in_specs=placed,
        out_specs=(P(("groups", "expert"), None), P(("groups", "expert"), None, None)),
        check_vma=False,
    )
```

```python
import functools

import jax
import jax.numpy as jnp
from jax import lax
from jax.experimental import pallas as pl
from jax.experimental.pallas import tpu as pltpu
from jax.sharding import PartitionSpec as P

PCAP = 1
PLANE = 4


LANES = 128


def sort_kernel(target_ref, pages_ref, out_ref):
    count, rows, width = pages_ref.shape
    if out_ref.shape[0] > count:
        out_ref[...] = jnp.full(out_ref.shape, -1.0, out_ref.dtype)

    @pl.loop(0, count)
    def _(p):
        target = target_ref[p]
        owner = target // count
        slot = (target - owner * count).astype(jnp.float32)
        out_ref[owner, :, :width] = pages_ref[p]
        out_ref[owner, :, width:] = jnp.full((rows, LANES), slot, jnp.float32).astype(jnp.bfloat16)


def sort_pages(kv_pages, page_target):
    count, rows, width = kv_pages.shape
    owners = lax.axis_size("expert")
    return pl.pallas_call(
        sort_kernel,
        out_shape=jax.ShapeDtypeStruct((owners * PCAP, rows, width + LANES), jnp.bfloat16),
        in_specs=[
            pl.BlockSpec(memory_space=pltpu.SMEM),
            pl.BlockSpec(memory_space=pltpu.VMEM),
        ],
        out_specs=pl.BlockSpec(memory_space=pltpu.VMEM),
        compiler_params=pltpu.CompilerParams(vmem_limit_bytes=16 * 2**20),
        cost_estimate=pl.CostEstimate(
            flops=0, bytes_accessed=6 * count * rows * width, transcendentals=0
        ),
    )(page_target, kv_pages)


def place_kernel(label_ref, arrived_ref, out_ref):
    sources = arrived_ref.shape[0]
    width = out_ref.shape[2]

    @pl.loop(0, sources)
    def _(p):
        label = label_ref[p]

        @pl.when((label >= 0) & (label < out_ref.shape[0]))
        def _():
            out_ref[label] = arrived_ref[p, :, :width]


def place_pages(arrived, page_shape):
    count, rows, width = page_shape
    labels = arrived[:, 0, width].astype(jnp.int32)
    return pl.pallas_call(
        place_kernel,
        out_shape=jax.ShapeDtypeStruct(page_shape, jnp.bfloat16),
        in_specs=[
            pl.BlockSpec(memory_space=pltpu.SMEM),
            pl.BlockSpec(memory_space=pltpu.VMEM),
        ],
        out_specs=pl.BlockSpec(memory_space=pltpu.VMEM),
        compiler_params=pltpu.CompilerParams(vmem_limit_bytes=16 * 2**20),
        cost_estimate=pl.CostEstimate(
            flops=0, bytes_accessed=4 * count * rows * width, transcendentals=0
        ),
    )(labels, arrived)


def exchange(x):
    return lax.all_to_all(x, "expert", split_axis=0, concat_axis=0, tiled=True)


def send(x, step=None, flip=None):
    count = lax.axis_size("expert")
    if flip is not None:
        pairs = [(i, i ^ flip) for i in range(count)]
    else:
        pairs = [(i, (i + step) % count) for i in range(count)]
    return lax.ppermute(x, "expert", pairs)


def after(x, *earlier):
    return lax.optimization_barrier((x, *earlier))[0]


def mixing_table(route_ids, route_gates, experts):
    shares = route_gates / jnp.sum(route_gates, axis=1, keepdims=True)
    mixing = shares.astype(jnp.bfloat16).astype(jnp.float32)
    hits = route_ids[:, :, None] == jnp.arange(experts, dtype=jnp.int32)
    return jnp.sum(jnp.where(hits, mixing[:, :, None], 0.0), axis=1).astype(jnp.bfloat16)


def spread(experts, capacity, chip):
    lane = lax.broadcasted_iota(jnp.int32, (experts, PLANE * capacity), 1)
    near = sum((lane >= capacity * j).astype(jnp.int32) for j in range(1, PLANE))
    near = (chip // PLANE) * PLANE + ((chip % PLANE) ^ near)
    expert = lax.broadcasted_iota(jnp.int32, (experts, PLANE * capacity), 0)
    return (expert == near).astype(jnp.float32).astype(jnp.bfloat16)


def slots_of(table, capacity, chip):
    rows, experts = table.shape
    weight = jnp.dot(table, spread(experts, capacity, chip), preferred_element_type=jnp.float32)
    named = weight > 0
    row = lax.broadcasted_iota(jnp.int32, (rows, rows), 0)
    below = (row > lax.broadcasted_iota(jnp.int32, (rows, rows), 1)).astype(jnp.float32)
    rank = jnp.dot(
        below.astype(jnp.bfloat16),
        named.astype(jnp.float32).astype(jnp.bfloat16),
        preferred_element_type=jnp.float32,
    )
    lane = lax.broadcasted_iota(jnp.int32, (rows, PLANE * capacity), 1)
    slot = lane - capacity * sum((lane >= capacity * j).astype(jnp.int32) for j in range(1, PLANE))
    hits = (rank == slot.astype(jnp.float32)) & named
    placing = jnp.where(hits, 1.0, 0.0).astype(jnp.bfloat16)
    blend = jnp.where(hits, weight, 0.0).astype(jnp.bfloat16)
    return placing, blend


def pick(placing, rows):
    return lax.dot_general(
        placing, rows, (((0,), (0,)), ((), ())), preferred_element_type=jnp.float32
    )


def pick_kernel(experts, capacity, step, chip_ref, block_ref, *outs):
    width = outs[0].shape[1]
    blend_ref = outs[PLANE - 1]
    placing, blend = slots_of(block_ref[:, width : width + experts], capacity, chip_ref[0])
    blend_ref[...] = blend
    for at in range(0, width, step):
        found = pick(placing, block_ref[:, at : at + step])
        for j in range(1, PLANE):
            part = found[capacity * j : capacity * (j + 1)]
            outs[j - 1][:, at : at + step] = part.astype(jnp.bfloat16)


def first_kernel(experts, capacity, step, chip_ref, tokens_ref, ids_ref, gates_ref, *outs):
    rows, width = tokens_ref.shape
    block_ref = outs[PLANE]
    ids = ids_ref[...].astype(jnp.float32).T.astype(jnp.int32)
    gates = gates_ref[...].T
    shares = gates / jnp.sum(gates, axis=1, keepdims=True)
    mixing = shares.astype(jnp.bfloat16).astype(jnp.float32)
    lane = lax.broadcasted_iota(jnp.int32, (rows, block_ref.shape[1] - width), 1)
    table = jnp.zeros(lane.shape, jnp.float32)
    for k in range(gates.shape[1]):
        table = table + jnp.where(ids[:, k : k + 1] == lane, mixing[:, k : k + 1], 0.0)
    block_ref[:, width:] = table.astype(jnp.bfloat16)
    block_ref[:, :width] = tokens_ref[...]
    pick_kernel(experts, capacity, step, chip_ref, block_ref, *outs[:PLANE])


def pick_pieces(chip, block, width, experts, capacity, routing=None):
    rows = block.shape[0]
    piece = jax.ShapeDtypeStruct((capacity, width), jnp.bfloat16)
    outs = [piece] * (PLANE - 1) + [jax.ShapeDtypeStruct((rows, PLANE * capacity), jnp.bfloat16)]
    if routing:
        lanes = experts + -experts % 128
        outs.append(jax.ShapeDtypeStruct((rows, width + lanes), jnp.bfloat16))
    body = first_kernel if routing else pick_kernel
    operands = (block, routing[0].T, routing[1].T) if routing else (block,)
    found = pl.pallas_call(
        functools.partial(body, experts, capacity, 512),
        out_shape=outs,
        in_specs=[pl.BlockSpec(memory_space=pltpu.SMEM)]
        + [pl.BlockSpec(memory_space=pltpu.VMEM)] * len(operands),
        out_specs=[pl.BlockSpec(memory_space=pltpu.VMEM)] * len(outs),
        compiler_params=pltpu.CompilerParams(vmem_limit_bytes=16 * 2**20),
        cost_estimate=pl.CostEstimate(
            flops=1200 * rows * PLANE * capacity * width,
            bytes_accessed=2 * width * (rows + PLANE * capacity),
            transcendentals=0,
        ),
    )(jnp.reshape(chip, (1,)), *operands)
    placing = (found[PLANE - 1][:, :capacity] > 0).astype(jnp.bfloat16)
    return [pick(placing, block[:, :width]).astype(jnp.bfloat16), *found]


def expert_kernel(pieces, steps, *refs):
    rows_in, weights = refs[:pieces], refs[pieces : pieces + 6]
    outs, hidden = refs[pieces + 6 : 2 * pieces + 6], refs[2 * pieces + 6]
    sums = refs[2 * pieces + 7 :]
    i = pl.program_id(0)
    half = hidden.shape[1] // 2

    @pl.when(i == 0)
    def _():
        for total in sums:
            total[...] = jnp.zeros_like(total)

    @pl.when(i < steps)
    def _():
        rows = jnp.concatenate([ref[...].astype(jnp.float32) for ref in rows_in], axis=0)
        rows = rows.astype(jnp.bfloat16)
        wide = jnp.concatenate([weight[...] for weight in weights[:4]], axis=1)
        found = jnp.dot(rows, wide, preferred_element_type=jnp.float32)
        for n, total in enumerate(sums):
            total[...] += found[:, n * half : (n + 1) * half]

    @pl.when(i == steps - 1)
    def _():
        for n in range(2):
            gate = sums[n][...]
            value = gate / (1.0 + jnp.exp(-gate)) * sums[2 + n][...]
            hidden[:, n * half : (n + 1) * half] = value.astype(jnp.bfloat16)

    @pl.when(i >= steps)
    def _():
        down = jnp.concatenate([weights[4][...], weights[5][...]], axis=0)
        out = jnp.dot(hidden[...], down, preferred_element_type=jnp.float32)
        each = out.shape[0] // pieces
        for n in range(pieces):
            outs[n][...] = out[n * each : (n + 1) * each].astype(jnp.bfloat16)


def apply(held, gate, up, down):
    pieces = [piece for arrived in held for piece in arrived]
    each, width = pieces[0].shape
    rows, half = each * len(pieces), gate[0].shape[1]
    step = 2048
    steps = width // step
    read = lambda i: jnp.minimum(i, steps - 1)
    write = lambda i: jnp.maximum(i - steps, 0)
    piece_in = pl.BlockSpec((each, step), lambda i: (0, read(i)))
    piece_out = pl.BlockSpec((each, step), lambda i: (0, write(i)))
    wide = pl.BlockSpec((step, half), lambda i: (read(i), 0))
    tall = pl.BlockSpec((half, step), lambda i: (0, write(i)))
    return pl.pallas_call(
        functools.partial(expert_kernel, len(pieces), steps),
        grid=(2 * steps,),
        out_shape=[jax.ShapeDtypeStruct((each, width), jnp.bfloat16)] * len(pieces),
        in_specs=[piece_in] * len(pieces) + [wide] * 4 + [tall] * 2,
        out_specs=[piece_out] * len(pieces),
        scratch_shapes=[pltpu.VMEM((rows, 2 * half), jnp.bfloat16)]
        + [pltpu.VMEM((rows, half), jnp.float32)] * 4,
        compiler_params=pltpu.CompilerParams(
            dimension_semantics=("arbitrary",), vmem_limit_bytes=60 * 2**20
        ),
        cost_estimate=pl.CostEstimate(
            flops=12 * rows * width * half,
            bytes_accessed=12 * width * half + 4 * rows * width,
            transcendentals=2 * rows * half,
        ),
    )(*pieces, *gate, *up, *down)


def apply_plain(held, gate, up, down):
    pieces = [piece for arrived in held for piece in arrived]
    rows = jnp.concatenate(pieces, axis=0)
    total = 0.0
    for n in range(2):
        left = jnp.dot(rows, gate[n], preferred_element_type=jnp.float32)
        right = jnp.dot(rows, up[n], preferred_element_type=jnp.float32)
        hidden = (jax.nn.silu(left) * right).astype(jnp.bfloat16)
        total = total + jnp.dot(hidden, down[n], preferred_element_type=jnp.float32)
    return jnp.split(total.astype(jnp.bfloat16), len(pieces), axis=0)


def pick_plain(chip, block, width, experts, capacity, routing=None):
    if routing:
        lanes = jnp.pad(mixing_table(*routing, experts), ((0, 0), (0, -experts % 128)))
        block = jnp.concatenate([block, lanes], axis=1)
    placing, blend = slots_of(block[:, width : width + experts], capacity, chip)
    found = pick(placing, block[:, :width]).astype(jnp.bfloat16)
    outs = jnp.split(found, PLANE, axis=0) + [blend]
    return outs + [block] if routing else outs


def local(
    tokens, route_ids, route_gates, gate_weight, up_weight, down_weight, kv_pages, page_target
):
    tok_rows, width = tokens.shape
    chosen = route_ids.shape[1]
    owners = lax.axis_size("expert")
    experts = owners // 2
    planes = experts // PLANE
    stride = 2 * PLANE
    capacity = min(tok_rows, 5 * tok_rows * chosen // (4 * experts))
    chip = lax.axis_index("expert") // 2
    whole = capacity % 8 == 0 and width % 2048 == 0
    choose, work = (pick_pieces, apply) if whole else (pick_plain, apply_plain)
    weights = (gate_weight, up_weight, down_weight)
    group = 2
    swapped, blends, got, outs = [], [], [], []
    outgoing = sort_pages(kv_pages, page_target)
    block = tokens
    for s in range(planes):
        if s:
            *pieces, blend = choose(chip, block, width, experts, capacity)
        else:
            *pieces, blend, block = choose(
                chip, tokens, width, experts, capacity, (route_ids, route_gates)
            )
        blends.append(blend)
        if s < 3:
            swapped.append(send(after(weights[s], *swapped, block), flip=1))
        for j in range(1, PLANE):
            piece = after(pieces[j], got[s - 1][j]) if s else pieces[j]
            pieces[j] = send(piece, flip=2 * j)
        got.append(pieces)
        if s + 1 < planes:
            block = send(block, step=stride)

    for first in range(0, planes, group):
        held = [list(pieces) for pieces in got[first : first + group]]
        following = got[first + group][1:] if first + group < planes else []
        held[0][0] = after(held[0][0], *outs, *following)
        outs.extend(work(held, *zip(weights, swapped)))

    arrived = exchange(after(outgoing, block))
    order = list(range(1, planes)) + [0]
    sent, landed = {}, got[-1][1:]
    for s in order:
        mine = outs[s * PLANE : (s + 1) * PLANE]
        sent[s] = [mine[0]]
        for j in range(1, PLANE):
            waits = [landed[-3 if s == 1 else -4]] + ([arrived] if s == 0 else [])
            landed.append(send(after(mine[j], *waits), flip=2 * j))
            sent[s].append(landed[-1])
    handed = place_pages(arrived, kv_pages.shape)
    sent[1][0] = after(sent[1][0], outs[-1])
    total = None
    for s in order:
        part = jnp.dot(
            blends[s], jnp.concatenate(sent[s], axis=0), preferred_element_type=jnp.float32
        )
        if total is not None:
            part = part + send(total, step=stride).astype(jnp.float32)
        total = part.astype(jnp.bfloat16)
    return (total, handed)


def solution(mesh):
    placed = (
        P(("groups", "expert"), None),
        P(("groups", "expert"), None),
        P(("groups", "expert"), None),
        P(None, "expert"),
        P(None, "expert"),
        P("expert", None),
        P(("groups", "expert"), None, None),
        P(("groups", "expert")),
    )
    return jax.shard_map(
        local,
        mesh=mesh,
        in_specs=placed,
        out_specs=(P(("groups", "expert"), None), P(("groups", "expert"), None, None)),
        check_vma=False,
    )
```

```python
import functools

import jax
import jax.numpy as jnp
from jax import lax
from jax.experimental import pallas as pl
from jax.experimental.pallas import tpu as pltpu
from jax.sharding import PartitionSpec as P

PCAP = 1
PLANE = 4


LANES = 128


def sort_kernel(target_ref, pages_ref, out_ref):
    count, rows, width = pages_ref.shape
    if out_ref.shape[0] > count:
        out_ref[...] = jnp.full(out_ref.shape, -1.0, out_ref.dtype)

    @pl.loop(0, count)
    def _(p):
        target = target_ref[p]
        owner = target // count
        slot = (target - owner * count).astype(jnp.float32)
        out_ref[owner, :, :width] = pages_ref[p]
        out_ref[owner, :, width:] = jnp.full((rows, LANES), slot, jnp.float32).astype(jnp.bfloat16)


def sort_pages(kv_pages, page_target):
    count, rows, width = kv_pages.shape
    owners = lax.axis_size("expert")
    return pl.pallas_call(
        sort_kernel,
        out_shape=jax.ShapeDtypeStruct((owners * PCAP, rows, width + LANES), jnp.bfloat16),
        in_specs=[
            pl.BlockSpec(memory_space=pltpu.SMEM),
            pl.BlockSpec(memory_space=pltpu.VMEM),
        ],
        out_specs=pl.BlockSpec(memory_space=pltpu.VMEM),
        compiler_params=pltpu.CompilerParams(vmem_limit_bytes=16 * 2**20),
        cost_estimate=pl.CostEstimate(
            flops=0, bytes_accessed=6 * count * rows * width, transcendentals=0
        ),
    )(page_target, kv_pages)


def place_kernel(label_ref, arrived_ref, out_ref):
    sources = arrived_ref.shape[0]
    width = out_ref.shape[2]

    @pl.loop(0, sources)
    def _(p):
        label = label_ref[p]

        @pl.when((label >= 0) & (label < out_ref.shape[0]))
        def _():
            out_ref[label] = arrived_ref[p, :, :width]


def place_pages(arrived, page_shape):
    count, rows, width = page_shape
    labels = arrived[:, 0, width].astype(jnp.int32)
    return pl.pallas_call(
        place_kernel,
        out_shape=jax.ShapeDtypeStruct(page_shape, jnp.bfloat16),
        in_specs=[
            pl.BlockSpec(memory_space=pltpu.SMEM),
            pl.BlockSpec(memory_space=pltpu.VMEM),
        ],
        out_specs=pl.BlockSpec(memory_space=pltpu.VMEM),
        compiler_params=pltpu.CompilerParams(vmem_limit_bytes=16 * 2**20),
        cost_estimate=pl.CostEstimate(
            flops=0, bytes_accessed=4 * count * rows * width, transcendentals=0
        ),
    )(labels, arrived)


def exchange(x):
    return lax.all_to_all(x, "expert", split_axis=0, concat_axis=0, tiled=True)


def send(x, step=None, flip=None):
    count = lax.axis_size("expert")
    if flip is not None:
        pairs = [(i, i ^ flip) for i in range(count)]
    else:
        pairs = [(i, (i + step) % count) for i in range(count)]
    return lax.ppermute(x, "expert", pairs)


def after(x, *earlier):
    return lax.optimization_barrier((x, *earlier))[0]


def mixing_table(route_ids, route_gates, experts):
    shares = route_gates / jnp.sum(route_gates, axis=1, keepdims=True)
    mixing = shares.astype(jnp.bfloat16).astype(jnp.float32)
    hits = route_ids[:, :, None] == jnp.arange(experts, dtype=jnp.int32)
    return jnp.sum(jnp.where(hits, mixing[:, :, None], 0.0), axis=1).astype(jnp.bfloat16)


def spread(experts, capacity, chip):
    lane = lax.broadcasted_iota(jnp.int32, (experts, PLANE * capacity), 1)
    near = sum((lane >= capacity * j).astype(jnp.int32) for j in range(1, PLANE))
    near = (chip // PLANE) * PLANE + ((chip % PLANE) ^ near)
    expert = lax.broadcasted_iota(jnp.int32, (experts, PLANE * capacity), 0)
    return (expert == near).astype(jnp.float32).astype(jnp.bfloat16)


def slots_of(table, capacity, chip):
    rows, experts = table.shape
    weight = jnp.dot(table, spread(experts, capacity, chip), preferred_element_type=jnp.float32)
    named = weight > 0
    row = lax.broadcasted_iota(jnp.int32, (rows, rows), 0)
    below = (row > lax.broadcasted_iota(jnp.int32, (rows, rows), 1)).astype(jnp.float32)
    rank = jnp.dot(
        below.astype(jnp.bfloat16),
        named.astype(jnp.float32).astype(jnp.bfloat16),
        preferred_element_type=jnp.float32,
    )
    lane = lax.broadcasted_iota(jnp.int32, (rows, PLANE * capacity), 1)
    slot = lane - capacity * sum((lane >= capacity * j).astype(jnp.int32) for j in range(1, PLANE))
    hits = (rank == slot.astype(jnp.float32)) & named
    placing = jnp.where(hits, 1.0, 0.0).astype(jnp.bfloat16)
    blend = jnp.where(hits, weight, 0.0).astype(jnp.bfloat16)
    return placing, blend


def pick(placing, rows):
    return lax.dot_general(
        placing, rows, (((0,), (0,)), ((), ())), preferred_element_type=jnp.float32
    )


def pick_kernel(experts, capacity, step, chip_ref, block_ref, *outs):
    width = outs[0].shape[1]
    blend_ref = outs[PLANE - 1]
    placing, blend = slots_of(block_ref[:, width : width + experts], capacity, chip_ref[0])
    blend_ref[...] = blend
    for at in range(0, width, step):
        found = pick(placing, block_ref[:, at : at + step])
        for j in range(1, PLANE):
            part = found[capacity * j : capacity * (j + 1)]
            outs[j - 1][:, at : at + step] = part.astype(jnp.bfloat16)


def first_kernel(experts, capacity, step, chip_ref, tokens_ref, ids_ref, gates_ref, *outs):
    rows, width = tokens_ref.shape
    block_ref = outs[PLANE]
    ids = ids_ref[...].astype(jnp.float32).T.astype(jnp.int32)
    gates = gates_ref[...].T
    shares = gates / jnp.sum(gates, axis=1, keepdims=True)
    mixing = shares.astype(jnp.bfloat16).astype(jnp.float32)
    lane = lax.broadcasted_iota(jnp.int32, (rows, block_ref.shape[1] - width), 1)
    table = jnp.zeros(lane.shape, jnp.float32)
    for k in range(gates.shape[1]):
        table = table + jnp.where(ids[:, k : k + 1] == lane, mixing[:, k : k + 1], 0.0)
    block_ref[:, width:] = table.astype(jnp.bfloat16)
    block_ref[:, :width] = tokens_ref[...]
    pick_kernel(experts, capacity, step, chip_ref, block_ref, *outs[:PLANE])


def pick_pieces(chip, block, width, experts, capacity, routing=None):
    rows = block.shape[0]
    piece = jax.ShapeDtypeStruct((capacity, width), jnp.bfloat16)
    outs = [piece] * (PLANE - 1) + [jax.ShapeDtypeStruct((rows, PLANE * capacity), jnp.bfloat16)]
    if routing:
        lanes = experts + -experts % 128
        outs.append(jax.ShapeDtypeStruct((rows, width + lanes), jnp.bfloat16))
    body = first_kernel if routing else pick_kernel
    operands = (block, routing[0].T, routing[1].T) if routing else (block,)
    found = pl.pallas_call(
        functools.partial(body, experts, capacity, 512),
        out_shape=outs,
        in_specs=[pl.BlockSpec(memory_space=pltpu.SMEM)]
        + [pl.BlockSpec(memory_space=pltpu.VMEM)] * len(operands),
        out_specs=[pl.BlockSpec(memory_space=pltpu.VMEM)] * len(outs),
        compiler_params=pltpu.CompilerParams(vmem_limit_bytes=16 * 2**20),
        cost_estimate=pl.CostEstimate(
            flops=1200 * rows * PLANE * capacity * width,
            bytes_accessed=2 * width * (rows + PLANE * capacity),
            transcendentals=0,
        ),
    )(jnp.reshape(chip, (1,)), *operands)
    placing = (found[PLANE - 1][:, :capacity] > 0).astype(jnp.bfloat16)
    return [pick(placing, block[:, :width]).astype(jnp.bfloat16), *found]


def expert_kernel(pieces, steps, *refs):
    rows_in, weights = refs[:pieces], refs[pieces : pieces + 6]
    outs, hidden = refs[pieces + 6 : 2 * pieces + 6], refs[2 * pieces + 6]
    sums = refs[2 * pieces + 7 :]
    i = pl.program_id(0)
    half = hidden.shape[1] // 2

    @pl.when(i == 0)
    def _():
        for total in sums:
            total[...] = jnp.zeros_like(total)

    @pl.when(i < steps)
    def _():
        rows = jnp.concatenate([ref[...].astype(jnp.float32) for ref in rows_in], axis=0)
        rows = rows.astype(jnp.bfloat16)
        wide = jnp.concatenate([weight[...] for weight in weights[:4]], axis=1)
        found = jnp.dot(rows, wide, preferred_element_type=jnp.float32)
        for n, total in enumerate(sums):
            total[...] += found[:, n * half : (n + 1) * half]

    @pl.when(i == steps - 1)
    def _():
        for n in range(2):
            gate = sums[n][...]
            value = gate / (1.0 + jnp.exp(-gate)) * sums[2 + n][...]
            hidden[:, n * half : (n + 1) * half] = value.astype(jnp.bfloat16)

    @pl.when(i >= steps)
    def _():
        down = jnp.concatenate([weights[4][...], weights[5][...]], axis=0)
        out = jnp.dot(hidden[...], down, preferred_element_type=jnp.float32)
        each = out.shape[0] // pieces
        for n in range(pieces):
            outs[n][...] = out[n * each : (n + 1) * each].astype(jnp.bfloat16)


def apply(held, gate, up, down):
    pieces = [piece for arrived in held for piece in arrived]
    each, width = pieces[0].shape
    rows, half = each * len(pieces), gate[0].shape[1]
    step = 2048
    steps = width // step
    read = lambda i: jnp.minimum(i, steps - 1)
    write = lambda i: jnp.maximum(i - steps, 0)
    piece_in = pl.BlockSpec((each, step), lambda i: (0, read(i)))
    piece_out = pl.BlockSpec((each, step), lambda i: (0, write(i)))
    wide = pl.BlockSpec((step, half), lambda i: (read(i), 0))
    tall = pl.BlockSpec((half, step), lambda i: (0, write(i)))
    return pl.pallas_call(
        functools.partial(expert_kernel, len(pieces), steps),
        grid=(2 * steps,),
        out_shape=[jax.ShapeDtypeStruct((each, width), jnp.bfloat16)] * len(pieces),
        in_specs=[piece_in] * len(pieces) + [wide] * 4 + [tall] * 2,
        out_specs=[piece_out] * len(pieces),
        scratch_shapes=[pltpu.VMEM((rows, 2 * half), jnp.bfloat16)]
        + [pltpu.VMEM((rows, half), jnp.float32)] * 4,
        compiler_params=pltpu.CompilerParams(
            dimension_semantics=("arbitrary",), vmem_limit_bytes=60 * 2**20
        ),
        cost_estimate=pl.CostEstimate(
            flops=12 * rows * width * half,
            bytes_accessed=12 * width * half + 4 * rows * width,
            transcendentals=2 * rows * half,
        ),
    )(*pieces, *gate, *up, *down)


def apply_plain(held, gate, up, down):
    pieces = [piece for arrived in held for piece in arrived]
    rows = jnp.concatenate(pieces, axis=0)
    total = 0.0
    for n in range(2):
        left = jnp.dot(rows, gate[n], preferred_element_type=jnp.float32)
        right = jnp.dot(rows, up[n], preferred_element_type=jnp.float32)
        hidden = (jax.nn.silu(left) * right).astype(jnp.bfloat16)
        total = total + jnp.dot(hidden, down[n], preferred_element_type=jnp.float32)
    return jnp.split(total.astype(jnp.bfloat16), len(pieces), axis=0)


def pick_plain(chip, block, width, experts, capacity, routing=None):
    if routing:
        lanes = jnp.pad(mixing_table(*routing, experts), ((0, 0), (0, -experts % 128)))
        block = jnp.concatenate([block, lanes], axis=1)
    placing, blend = slots_of(block[:, width : width + experts], capacity, chip)
    found = pick(placing, block[:, :width]).astype(jnp.bfloat16)
    outs = jnp.split(found, PLANE, axis=0) + [blend]
    return outs + [block] if routing else outs


def local(
    tokens, route_ids, route_gates, gate_weight, up_weight, down_weight, kv_pages, page_target
):
    tok_rows, width = tokens.shape
    chosen = route_ids.shape[1]
    owners = lax.axis_size("expert")
    experts = owners // 2
    planes = experts // PLANE
    stride = 2 * PLANE
    capacity = min(tok_rows, 5 * tok_rows * chosen // (4 * experts))
    chip = lax.axis_index("expert") // 2
    whole = capacity % 8 == 0 and width % 2048 == 0
    choose, work = (pick_pieces, apply) if whole else (pick_plain, apply_plain)
    weights = (gate_weight, up_weight, down_weight)
    group = 2
    swapped, blends, got, outs = [], [], [], []
    outgoing = sort_pages(kv_pages, page_target)
    block = tokens
    for s in range(planes):
        if s:
            *pieces, blend = choose(chip, block, width, experts, capacity)
        else:
            *pieces, blend, block = choose(
                chip, tokens, width, experts, capacity, (route_ids, route_gates)
            )
        blends.append(blend)
        if s < 3:
            swapped.append(send(after(weights[s], *swapped, block), flip=1))
        for j in range(1, PLANE):
            piece = after(pieces[j], got[s - 1][j]) if s else pieces[j]
            pieces[j] = send(piece, flip=2 * j)
        got.append(pieces)
        if s + 1 < planes:
            block = send(block, step=stride)

    for first in range(0, planes, group):
        held = [list(pieces) for pieces in got[first : first + group]]
        held[0][0] = after(held[0][0], *outs)
        outs.extend(work(held, *zip(weights, swapped)))

    arrived = exchange(after(outgoing, block))
    order = list(range(1, planes)) + [0]
    sent, landed = {}, got[-1][1:]
    for s in order:
        mine = outs[s * PLANE : (s + 1) * PLANE]
        sent[s] = [mine[0]]
        for j in range(1, PLANE):
            waits = [landed[-3 if s == 1 else -4]] + ([arrived] if s == 0 else [])
            landed.append(send(after(mine[j], *waits), flip=2 * j))
            sent[s].append(landed[-1])
    handed = place_pages(arrived, kv_pages.shape)
    sent[1][0] = after(sent[1][0], outs[-1])
    total = None
    for s in order:
        part = jnp.dot(
            blends[s], jnp.concatenate(sent[s], axis=0), preferred_element_type=jnp.float32
        )
        if total is not None:
            part = part + send(total, step=stride).astype(jnp.float32)
        total = part.astype(jnp.bfloat16)
    return (total, handed)


def solution(mesh):
    placed = (
        P(("groups", "expert"), None),
        P(("groups", "expert"), None),
        P(("groups", "expert"), None),
        P(None, "expert"),
        P(None, "expert"),
        P("expert", None),
        P(("groups", "expert"), None, None),
        P(("groups", "expert")),
    )
    return jax.shard_map(
        local,
        mesh=mesh,
        in_specs=placed,
        out_specs=(P(("groups", "expert"), None), P(("groups", "expert"), None, None)),
        check_vma=False,
    )
```

```python
import functools

import jax
import jax.numpy as jnp
from jax import lax
from jax.experimental import pallas as pl
from jax.experimental.pallas import tpu as pltpu
from jax.sharding import PartitionSpec as P

PCAP = 1
PLANE = 4


LANES = 128


def sort_kernel(target_ref, pages_ref, out_ref):
    count, rows, width = pages_ref.shape
    if out_ref.shape[0] > count:
        out_ref[...] = jnp.full(out_ref.shape, -1.0, out_ref.dtype)

    @pl.loop(0, count)
    def _(p):
        target = target_ref[p]
        owner = target // count
        slot = (target - owner * count).astype(jnp.float32)
        out_ref[owner, :, :width] = pages_ref[p]
        out_ref[owner, :, width:] = jnp.full((rows, LANES), slot, jnp.float32).astype(jnp.bfloat16)


def sort_pages(kv_pages, page_target):
    count, rows, width = kv_pages.shape
    owners = lax.axis_size("expert")
    return pl.pallas_call(
        sort_kernel,
        out_shape=jax.ShapeDtypeStruct((owners * PCAP, rows, width + LANES), jnp.bfloat16),
        in_specs=[
            pl.BlockSpec(memory_space=pltpu.SMEM),
            pl.BlockSpec(memory_space=pltpu.VMEM),
        ],
        out_specs=pl.BlockSpec(memory_space=pltpu.VMEM),
        compiler_params=pltpu.CompilerParams(vmem_limit_bytes=16 * 2**20),
        cost_estimate=pl.CostEstimate(
            flops=0, bytes_accessed=6 * count * rows * width, transcendentals=0
        ),
    )(page_target, kv_pages)


def place_kernel(label_ref, arrived_ref, out_ref):
    sources = arrived_ref.shape[0]
    width = out_ref.shape[2]

    @pl.loop(0, sources)
    def _(p):
        label = label_ref[p]

        @pl.when((label >= 0) & (label < out_ref.shape[0]))
        def _():
            out_ref[label] = arrived_ref[p, :, :width]


def place_pages(arrived, page_shape):
    count, rows, width = page_shape
    labels = arrived[:, 0, width].astype(jnp.int32)
    return pl.pallas_call(
        place_kernel,
        out_shape=jax.ShapeDtypeStruct(page_shape, jnp.bfloat16),
        in_specs=[
            pl.BlockSpec(memory_space=pltpu.SMEM),
            pl.BlockSpec(memory_space=pltpu.VMEM),
        ],
        out_specs=pl.BlockSpec(memory_space=pltpu.VMEM),
        compiler_params=pltpu.CompilerParams(vmem_limit_bytes=16 * 2**20),
        cost_estimate=pl.CostEstimate(
            flops=0, bytes_accessed=4 * count * rows * width, transcendentals=0
        ),
    )(labels, arrived)


def exchange(x):
    return lax.all_to_all(x, "expert", split_axis=0, concat_axis=0, tiled=True)


def send(x, step=None, flip=None):
    count = lax.axis_size("expert")
    if flip is not None:
        pairs = [(i, i ^ flip) for i in range(count)]
    else:
        pairs = [(i, (i + step) % count) for i in range(count)]
    return lax.ppermute(x, "expert", pairs)


def after(x, *earlier):
    return lax.optimization_barrier((x, *earlier))[0]


def mixing_table(route_ids, route_gates, experts):
    shares = route_gates / jnp.sum(route_gates, axis=1, keepdims=True)
    mixing = shares.astype(jnp.bfloat16).astype(jnp.float32)
    hits = route_ids[:, :, None] == jnp.arange(experts, dtype=jnp.int32)
    return jnp.sum(jnp.where(hits, mixing[:, :, None], 0.0), axis=1).astype(jnp.bfloat16)


def spread(experts, capacity, chip):
    lane = lax.broadcasted_iota(jnp.int32, (experts, PLANE * capacity), 1)
    near = sum((lane >= capacity * j).astype(jnp.int32) for j in range(1, PLANE))
    near = (chip // PLANE) * PLANE + ((chip % PLANE) ^ near)
    expert = lax.broadcasted_iota(jnp.int32, (experts, PLANE * capacity), 0)
    return (expert == near).astype(jnp.float32).astype(jnp.bfloat16)


def slots_of(table, capacity, chip):
    rows, experts = table.shape
    weight = jnp.dot(table, spread(experts, capacity, chip), preferred_element_type=jnp.float32)
    named = weight > 0
    row = lax.broadcasted_iota(jnp.int32, (rows, rows), 0)
    below = (row > lax.broadcasted_iota(jnp.int32, (rows, rows), 1)).astype(jnp.float32)
    rank = jnp.dot(
        below.astype(jnp.bfloat16),
        named.astype(jnp.float32).astype(jnp.bfloat16),
        preferred_element_type=jnp.float32,
    )
    lane = lax.broadcasted_iota(jnp.int32, (rows, PLANE * capacity), 1)
    slot = lane - capacity * sum((lane >= capacity * j).astype(jnp.int32) for j in range(1, PLANE))
    hits = (rank == slot.astype(jnp.float32)) & named
    placing = jnp.where(hits, 1.0, 0.0).astype(jnp.bfloat16)
    blend = jnp.where(hits, weight, 0.0).astype(jnp.bfloat16)
    return placing, blend


def pick(placing, rows):
    return lax.dot_general(
        placing, rows, (((0,), (0,)), ((), ())), preferred_element_type=jnp.float32
    )


def pick_kernel(experts, capacity, step, chip_ref, block_ref, *outs):
    width = outs[0].shape[1]
    blend_ref = outs[PLANE - 1]
    placing, blend = slots_of(block_ref[:, width : width + experts], capacity, chip_ref[0])
    blend_ref[...] = blend
    for at in range(0, width, step):
        found = pick(placing, block_ref[:, at : at + step])
        for j in range(1, PLANE):
            part = found[capacity * j : capacity * (j + 1)]
            outs[j - 1][:, at : at + step] = part.astype(jnp.bfloat16)


def first_kernel(experts, capacity, step, chip_ref, tokens_hbm, ids_hbm, gates_hbm, *outs):
    rows, width = tokens_hbm.shape
    block_ref, ids_ref, gates_ref, sems = outs[PLANE:]
    ids_copy = pltpu.make_async_copy(ids_hbm, ids_ref, sems.at[0])
    gates_copy = pltpu.make_async_copy(gates_hbm, gates_ref, sems.at[1])
    tokens_copy = pltpu.make_async_copy(tokens_hbm, block_ref.at[:, :width], sems.at[2])
    ids_copy.start()
    gates_copy.start()
    tokens_copy.start()
    ids_copy.wait()
    gates_copy.wait()
    ids = ids_ref[...].astype(jnp.float32).T.astype(jnp.int32)
    gates = gates_ref[...].T
    shares = gates / jnp.sum(gates, axis=1, keepdims=True)
    mixing = shares.astype(jnp.bfloat16).astype(jnp.float32)
    lane = lax.broadcasted_iota(jnp.int32, (rows, block_ref.shape[1] - width), 1)
    table = jnp.zeros(lane.shape, jnp.float32)
    for k in range(gates.shape[1]):
        table = table + jnp.where(ids[:, k : k + 1] == lane, mixing[:, k : k + 1], 0.0)
    block_ref[:, width:] = table.astype(jnp.bfloat16)
    tokens_copy.wait()
    pick_kernel(experts, capacity, step, chip_ref, block_ref, *outs[:PLANE])


def pick_pieces(chip, block, width, experts, capacity, routing=None):
    rows = block.shape[0]
    piece = jax.ShapeDtypeStruct((capacity, width), jnp.bfloat16)
    outs = [piece] * (PLANE - 1) + [jax.ShapeDtypeStruct((rows, PLANE * capacity), jnp.bfloat16)]
    if routing:
        lanes = experts + -experts % 128
        outs.append(jax.ShapeDtypeStruct((rows, width + lanes), jnp.bfloat16))
    body = first_kernel if routing else pick_kernel
    operands = (block, routing[0].T, routing[1].T) if routing else (block,)
    space = pl.ANY if routing else pltpu.VMEM
    found = pl.pallas_call(
        functools.partial(body, experts, capacity, 512),
        out_shape=outs,
        in_specs=[pl.BlockSpec(memory_space=pltpu.SMEM)]
        + [pl.BlockSpec(memory_space=space)] * len(operands),
        scratch_shapes=[
            pltpu.VMEM(operands[1].shape, jnp.int32),
            pltpu.VMEM(operands[2].shape, jnp.float32),
            pltpu.SemaphoreType.DMA((3,)),
        ]
        if routing
        else [],
        out_specs=[pl.BlockSpec(memory_space=pltpu.VMEM)] * len(outs),
        compiler_params=pltpu.CompilerParams(vmem_limit_bytes=(60 if routing else 16) * 2**20),
        cost_estimate=pl.CostEstimate(
            flops=1200 * rows * PLANE * capacity * width,
            bytes_accessed=2 * width * (rows + PLANE * capacity),
            transcendentals=0,
        ),
    )(jnp.reshape(chip, (1,)), *operands)
    placing = (found[PLANE - 1][:, :capacity] > 0).astype(jnp.bfloat16)
    return [pick(placing, block[:, :width]).astype(jnp.bfloat16), *found]


def expert_kernel(pieces, steps, *refs):
    rows_in, weights = refs[:pieces], refs[pieces : pieces + 6]
    outs, hidden = refs[pieces + 6 : 2 * pieces + 6], refs[2 * pieces + 6]
    sums = refs[2 * pieces + 7 :]
    i = pl.program_id(0)
    half = hidden.shape[1] // 2

    @pl.when(i == 0)
    def _():
        for total in sums:
            total[...] = jnp.zeros_like(total)

    @pl.when(i < steps)
    def _():
        rows = jnp.concatenate([ref[...].astype(jnp.float32) for ref in rows_in], axis=0)
        rows = rows.astype(jnp.bfloat16)
        wide = jnp.concatenate([weight[...] for weight in weights[:4]], axis=1)
        found = jnp.dot(rows, wide, preferred_element_type=jnp.float32)
        for n, total in enumerate(sums):
            total[...] += found[:, n * half : (n + 1) * half]

    @pl.when(i == steps - 1)
    def _():
        for n in range(2):
            gate = sums[n][...]
            value = gate / (1.0 + jnp.exp(-gate)) * sums[2 + n][...]
            hidden[:, n * half : (n + 1) * half] = value.astype(jnp.bfloat16)

    @pl.when(i >= steps)
    def _():
        down = jnp.concatenate([weights[4][...], weights[5][...]], axis=0)
        out = jnp.dot(hidden[...], down, preferred_element_type=jnp.float32)
        each = out.shape[0] // pieces
        for n in range(pieces):
            outs[n][...] = out[n * each : (n + 1) * each].astype(jnp.bfloat16)


def apply(held, gate, up, down):
    pieces = [piece for arrived in held for piece in arrived]
    each, width = pieces[0].shape
    rows, half = each * len(pieces), gate[0].shape[1]
    step = 2048
    steps = width // step
    read = lambda i: jnp.minimum(i, steps - 1)
    write = lambda i: jnp.maximum(i - steps, 0)
    piece_in = pl.BlockSpec((each, step), lambda i: (0, read(i)))
    piece_out = pl.BlockSpec((each, step), lambda i: (0, write(i)))
    wide = pl.BlockSpec((step, half), lambda i: (read(i), 0))
    tall = pl.BlockSpec((half, step), lambda i: (0, write(i)))
    return pl.pallas_call(
        functools.partial(expert_kernel, len(pieces), steps),
        grid=(2 * steps,),
        out_shape=[jax.ShapeDtypeStruct((each, width), jnp.bfloat16)] * len(pieces),
        in_specs=[piece_in] * len(pieces) + [wide] * 4 + [tall] * 2,
        out_specs=[piece_out] * len(pieces),
        scratch_shapes=[pltpu.VMEM((rows, 2 * half), jnp.bfloat16)]
        + [pltpu.VMEM((rows, half), jnp.float32)] * 4,
        compiler_params=pltpu.CompilerParams(
            dimension_semantics=("arbitrary",), vmem_limit_bytes=60 * 2**20
        ),
        cost_estimate=pl.CostEstimate(
            flops=12 * rows * width * half,
            bytes_accessed=12 * width * half + 4 * rows * width,
            transcendentals=2 * rows * half,
        ),
    )(*pieces, *gate, *up, *down)


def apply_plain(held, gate, up, down):
    pieces = [piece for arrived in held for piece in arrived]
    rows = jnp.concatenate(pieces, axis=0)
    total = 0.0
    for n in range(2):
        left = jnp.dot(rows, gate[n], preferred_element_type=jnp.float32)
        right = jnp.dot(rows, up[n], preferred_element_type=jnp.float32)
        hidden = (jax.nn.silu(left) * right).astype(jnp.bfloat16)
        total = total + jnp.dot(hidden, down[n], preferred_element_type=jnp.float32)
    return jnp.split(total.astype(jnp.bfloat16), len(pieces), axis=0)


def pick_plain(chip, block, width, experts, capacity, routing=None):
    if routing:
        lanes = jnp.pad(mixing_table(*routing, experts), ((0, 0), (0, -experts % 128)))
        block = jnp.concatenate([block, lanes], axis=1)
    placing, blend = slots_of(block[:, width : width + experts], capacity, chip)
    found = pick(placing, block[:, :width]).astype(jnp.bfloat16)
    outs = jnp.split(found, PLANE, axis=0) + [blend]
    return outs + [block] if routing else outs


def local(
    tokens, route_ids, route_gates, gate_weight, up_weight, down_weight, kv_pages, page_target
):
    tok_rows, width = tokens.shape
    chosen = route_ids.shape[1]
    owners = lax.axis_size("expert")
    experts = owners // 2
    planes = experts // PLANE
    stride = 2 * PLANE
    capacity = min(tok_rows, 5 * tok_rows * chosen // (4 * experts))
    chip = lax.axis_index("expert") // 2
    whole = capacity % 8 == 0 and width % 2048 == 0
    choose, work = (pick_pieces, apply) if whole else (pick_plain, apply_plain)
    weights = (gate_weight, up_weight, down_weight)
    group = 2
    swapped, blends, got, outs = [], [], [], []
    outgoing = sort_pages(kv_pages, page_target)
    block = tokens
    for s in range(planes):
        if s:
            *pieces, blend = choose(chip, block, width, experts, capacity)
        else:
            *pieces, blend, block = choose(
                chip, tokens, width, experts, capacity, (route_ids, route_gates)
            )
        blends.append(blend)
        if s < 3:
            swapped.append(send(after(weights[s], *swapped, block), flip=1))
        for j in range(1, PLANE):
            piece = after(pieces[j], got[s - 1][j]) if s else pieces[j]
            pieces[j] = send(piece, flip=2 * j)
        got.append(pieces)
        if s + 1 < planes:
            block = send(block, step=stride)

    for first in range(0, planes, group):
        held = [list(pieces) for pieces in got[first : first + group]]
        held[0][0] = after(held[0][0], *outs)
        outs.extend(work(held, *zip(weights, swapped)))

    arrived = exchange(after(outgoing, block))
    order = list(range(1, planes)) + [0]
    sent, landed = {}, got[-1][1:]
    for s in order:
        mine = outs[s * PLANE : (s + 1) * PLANE]
        sent[s] = [mine[0]]
        for j in range(1, PLANE):
            waits = [landed[-3 if s == 1 else -4]] + ([arrived] if s == 0 else [])
            landed.append(send(after(mine[j], *waits), flip=2 * j))
            sent[s].append(landed[-1])
    handed = place_pages(arrived, kv_pages.shape)
    sent[1][0] = after(sent[1][0], outs[-1])
    total = None
    for s in order:
        part = jnp.dot(
            blends[s], jnp.concatenate(sent[s], axis=0), preferred_element_type=jnp.float32
        )
        if total is not None:
            part = part + send(total, step=stride).astype(jnp.float32)
        total = part.astype(jnp.bfloat16)
    return (total, handed)


def solution(mesh):
    placed = (
        P(("groups", "expert"), None),
        P(("groups", "expert"), None),
        P(("groups", "expert"), None),
        P(None, "expert"),
        P(None, "expert"),
        P("expert", None),
        P(("groups", "expert"), None, None),
        P(("groups", "expert")),
    )
    return jax.shard_map(
        local,
        mesh=mesh,
        in_specs=placed,
        out_specs=(P(("groups", "expert"), None), P(("groups", "expert"), None, None)),
        check_vma=False,
    )
```

```python
import functools

import jax
import jax.numpy as jnp
from jax import lax
from jax.experimental import pallas as pl
from jax.experimental.pallas import tpu as pltpu
from jax.sharding import PartitionSpec as P

PCAP = 1
PLANE = 4


LANES = 128


def sort_kernel(target_ref, pages_ref, out_ref):
    count, rows, width = pages_ref.shape
    if out_ref.shape[0] > count:
        out_ref[...] = jnp.full(out_ref.shape, -1.0, out_ref.dtype)

    @pl.loop(0, count)
    def _(p):
        target = target_ref[p]
        owner = target // count
        slot = (target - owner * count).astype(jnp.float32)
        out_ref[owner, :, :width] = pages_ref[p]
        out_ref[owner, :, width:] = jnp.full((rows, LANES), slot, jnp.float32).astype(jnp.bfloat16)


def sort_pages(kv_pages, page_target):
    count, rows, width = kv_pages.shape
    owners = lax.axis_size("expert")
    return pl.pallas_call(
        sort_kernel,
        out_shape=jax.ShapeDtypeStruct((owners * PCAP, rows, width + LANES), jnp.bfloat16),
        in_specs=[
            pl.BlockSpec(memory_space=pltpu.SMEM),
            pl.BlockSpec(memory_space=pltpu.VMEM),
        ],
        out_specs=pl.BlockSpec(memory_space=pltpu.VMEM),
        compiler_params=pltpu.CompilerParams(vmem_limit_bytes=16 * 2**20),
        cost_estimate=pl.CostEstimate(
            flops=0, bytes_accessed=6 * count * rows * width, transcendentals=0
        ),
    )(page_target, kv_pages)


def place_kernel(label_ref, arrived_ref, out_ref):
    sources = arrived_ref.shape[0]
    width = out_ref.shape[2]

    @pl.loop(0, sources)
    def _(p):
        label = label_ref[p]

        @pl.when((label >= 0) & (label < out_ref.shape[0]))
        def _():
            out_ref[label] = arrived_ref[p, :, :width]


def place_pages(arrived, page_shape):
    count, rows, width = page_shape
    labels = arrived[:, 0, width].astype(jnp.int32)
    return pl.pallas_call(
        place_kernel,
        out_shape=jax.ShapeDtypeStruct(page_shape, jnp.bfloat16),
        in_specs=[
            pl.BlockSpec(memory_space=pltpu.SMEM),
            pl.BlockSpec(memory_space=pltpu.VMEM),
        ],
        out_specs=pl.BlockSpec(memory_space=pltpu.VMEM),
        compiler_params=pltpu.CompilerParams(vmem_limit_bytes=16 * 2**20),
        cost_estimate=pl.CostEstimate(
            flops=0, bytes_accessed=4 * count * rows * width, transcendentals=0
        ),
    )(labels, arrived)


def exchange(x):
    return lax.all_to_all(x, "expert", split_axis=0, concat_axis=0, tiled=True)


def send(x, step=None, flip=None):
    count = lax.axis_size("expert")
    if flip is not None:
        pairs = [(i, i ^ flip) for i in range(count)]
    else:
        pairs = [(i, (i + step) % count) for i in range(count)]
    return lax.ppermute(x, "expert", pairs)


def after(x, *earlier):
    return lax.optimization_barrier((x, *earlier))[0]


def mixing_table(route_ids, route_gates, experts):
    shares = route_gates / jnp.sum(route_gates, axis=1, keepdims=True)
    mixing = shares.astype(jnp.bfloat16).astype(jnp.float32)
    hits = route_ids[:, :, None] == jnp.arange(experts, dtype=jnp.int32)
    return jnp.sum(jnp.where(hits, mixing[:, :, None], 0.0), axis=1).astype(jnp.bfloat16)


def spread(experts, capacity, chip):
    lane = lax.broadcasted_iota(jnp.int32, (experts, PLANE * capacity), 1)
    near = sum((lane >= capacity * j).astype(jnp.int32) for j in range(1, PLANE))
    near = (chip // PLANE) * PLANE + ((chip % PLANE) ^ near)
    expert = lax.broadcasted_iota(jnp.int32, (experts, PLANE * capacity), 0)
    return (expert == near).astype(jnp.float32).astype(jnp.bfloat16)


def slots_of(table, capacity, chip):
    rows, experts = table.shape
    weight = jnp.dot(table, spread(experts, capacity, chip), preferred_element_type=jnp.float32)
    named = weight > 0
    row = lax.broadcasted_iota(jnp.int32, (rows, rows), 0)
    below = (row > lax.broadcasted_iota(jnp.int32, (rows, rows), 1)).astype(jnp.float32)
    rank = jnp.dot(
        below.astype(jnp.bfloat16),
        named.astype(jnp.float32).astype(jnp.bfloat16),
        preferred_element_type=jnp.float32,
    )
    lane = lax.broadcasted_iota(jnp.int32, (rows, PLANE * capacity), 1)
    slot = lane - capacity * sum((lane >= capacity * j).astype(jnp.int32) for j in range(1, PLANE))
    hits = (rank == slot.astype(jnp.float32)) & named
    placing = jnp.where(hits, 1.0, 0.0).astype(jnp.bfloat16)
    blend = jnp.where(hits, weight, 0.0).astype(jnp.bfloat16)
    return placing, blend


def pick(placing, rows):
    return lax.dot_general(
        placing, rows, (((0,), (0,)), ((), ())), preferred_element_type=jnp.float32
    )


def pick_kernel(experts, capacity, step, chip_ref, block_ref, *outs):
    width = outs[0].shape[1]
    blend_ref = outs[PLANE - 1]
    placing, blend = slots_of(block_ref[:, width : width + experts], capacity, chip_ref[0])
    blend_ref[...] = blend
    for at in range(0, width, step):
        found = pick(placing, block_ref[:, at : at + step])
        for j in range(1, PLANE):
            part = found[capacity * j : capacity * (j + 1)]
            outs[j - 1][:, at : at + step] = part.astype(jnp.bfloat16)


def first_kernel(experts, capacity, step, chip_ref, tokens_hbm, ids_hbm, gates_hbm, *outs):
    rows, width = tokens_hbm.shape
    block_ref, ids_ref, gates_ref, sems = outs[PLANE:]
    ids_copy = pltpu.make_async_copy(ids_hbm, ids_ref, sems.at[0])
    gates_copy = pltpu.make_async_copy(gates_hbm, gates_ref, sems.at[1])
    tokens_copy = pltpu.make_async_copy(tokens_hbm, block_ref.at[:, :width], sems.at[2])
    ids_copy.start()
    gates_copy.start()
    tokens_copy.start()
    ids_copy.wait()
    gates_copy.wait()
    ids = ids_ref[...].astype(jnp.float32).T.astype(jnp.int32)
    gates = gates_ref[...].T
    shares = gates / jnp.sum(gates, axis=1, keepdims=True)
    mixing = shares.astype(jnp.bfloat16).astype(jnp.float32)
    lane = lax.broadcasted_iota(jnp.int32, (rows, block_ref.shape[1] - width), 1)
    table = jnp.zeros(lane.shape, jnp.float32)
    for k in range(gates.shape[1]):
        table = table + jnp.where(ids[:, k : k + 1] == lane, mixing[:, k : k + 1], 0.0)
    block_ref[:, width:] = table.astype(jnp.bfloat16)
    tokens_copy.wait()
    pick_kernel(experts, capacity, step, chip_ref, block_ref, *outs[:PLANE])


def pick_pieces(chip, block, width, experts, capacity, routing=None):
    rows = block.shape[0]
    piece = jax.ShapeDtypeStruct((capacity, width), jnp.bfloat16)
    outs = [piece] * (PLANE - 1) + [jax.ShapeDtypeStruct((rows, PLANE * capacity), jnp.bfloat16)]
    if routing:
        lanes = experts + -experts % 128
        outs.append(jax.ShapeDtypeStruct((rows, width + lanes), jnp.bfloat16))
    body = first_kernel if routing else pick_kernel
    operands = (block, routing[0].T, routing[1].T) if routing else (block,)
    space = pl.ANY if routing else pltpu.VMEM
    found = pl.pallas_call(
        functools.partial(body, experts, capacity, 512),
        out_shape=outs,
        in_specs=[pl.BlockSpec(memory_space=pltpu.SMEM)]
        + [pl.BlockSpec(memory_space=space)] * len(operands),
        scratch_shapes=[
            pltpu.VMEM(operands[1].shape, jnp.int32),
            pltpu.VMEM(operands[2].shape, jnp.float32),
            pltpu.SemaphoreType.DMA((3,)),
        ]
        if routing
        else [],
        out_specs=[pl.BlockSpec(memory_space=pltpu.VMEM)] * len(outs),
        compiler_params=pltpu.CompilerParams(vmem_limit_bytes=(60 if routing else 16) * 2**20),
        cost_estimate=pl.CostEstimate(
            flops=1200 * rows * PLANE * capacity * width,
            bytes_accessed=2 * width * (rows + PLANE * capacity),
            transcendentals=0,
        ),
    )(jnp.reshape(chip, (1,)), *operands)
    placing = (found[PLANE - 1][:, :capacity] > 0).astype(jnp.bfloat16)
    return [pick(placing, block[:, :width]).astype(jnp.bfloat16), *found]


def expert_kernel(pieces, steps, *refs):
    rows_in, weights = refs[:pieces], refs[pieces : pieces + 6]
    outs, hidden = refs[pieces + 6 : 2 * pieces + 6], refs[2 * pieces + 6]
    sums = refs[2 * pieces + 7 :]
    i = pl.program_id(0)
    half = hidden.shape[1] // 2

    @pl.when(i == 0)
    def _():
        for total in sums:
            total[...] = jnp.zeros_like(total)

    @pl.when(i < steps)
    def _():
        rows = jnp.concatenate([ref[...].astype(jnp.float32) for ref in rows_in], axis=0)
        rows = rows.astype(jnp.bfloat16)
        wide = jnp.concatenate([weight[...] for weight in weights[:4]], axis=1)
        found = jnp.dot(rows, wide, preferred_element_type=jnp.float32)
        for n, total in enumerate(sums):
            total[...] += found[:, n * half : (n + 1) * half]

    @pl.when(i == steps - 1)
    def _():
        for n in range(2):
            gate = sums[n][...]
            value = gate / (1.0 + jnp.exp(-gate)) * sums[2 + n][...]
            hidden[:, n * half : (n + 1) * half] = value.astype(jnp.bfloat16)

    @pl.when(i >= steps)
    def _():
        down = jnp.concatenate([weights[4][...], weights[5][...]], axis=0)
        out = jnp.dot(hidden[...], down, preferred_element_type=jnp.float32)
        each = out.shape[0] // pieces
        for n in range(pieces):
            outs[n][...] = out[n * each : (n + 1) * each].astype(jnp.bfloat16)


def apply(held, gate, up, down):
    pieces = [piece for arrived in held for piece in arrived]
    each, width = pieces[0].shape
    rows, half = each * len(pieces), gate[0].shape[1]
    step = 2048
    steps = width // step
    read = lambda i: jnp.minimum(i, steps - 1)
    write = lambda i: jnp.maximum(i - steps, 0)
    piece_in = pl.BlockSpec((each, step), lambda i: (0, read(i)))
    piece_out = pl.BlockSpec((each, step), lambda i: (0, write(i)))
    wide = pl.BlockSpec((step, half), lambda i: (read(i), 0))
    tall = pl.BlockSpec((half, step), lambda i: (0, write(i)))
    return pl.pallas_call(
        functools.partial(expert_kernel, len(pieces), steps),
        grid=(2 * steps,),
        out_shape=[jax.ShapeDtypeStruct((each, width), jnp.bfloat16)] * len(pieces),
        in_specs=[piece_in] * len(pieces) + [wide] * 4 + [tall] * 2,
        out_specs=[piece_out] * len(pieces),
        scratch_shapes=[pltpu.VMEM((rows, 2 * half), jnp.bfloat16)]
        + [pltpu.VMEM((rows, half), jnp.float32)] * 4,
        compiler_params=pltpu.CompilerParams(
            dimension_semantics=("arbitrary",), vmem_limit_bytes=60 * 2**20
        ),
        cost_estimate=pl.CostEstimate(
            flops=12 * rows * width * half,
            bytes_accessed=12 * width * half + 4 * rows * width,
            transcendentals=2 * rows * half,
        ),
    )(*pieces, *gate, *up, *down)


def blend_kernel(blend_ref, *refs):
    *inputs, out_ref = refs
    pieces, earlier = inputs[:PLANE], inputs[PLANE:]
    step = 512
    for at in range(0, out_ref.shape[1], step):
        rows = [ref[:, at : at + step].astype(jnp.float32) for ref in pieces]
        rows = jnp.concatenate(rows, axis=0).astype(jnp.bfloat16)
        total = jnp.dot(blend_ref[...], rows, preferred_element_type=jnp.float32)
        for ref in earlier:
            total = total + ref[:, at : at + step].astype(jnp.float32)
        out_ref[:, at : at + step] = total


def blend_pieces(blend, pieces, earlier):
    rows, width = blend.shape[0], pieces[0].shape[1]
    operands = (blend, *pieces, *earlier)
    return pl.pallas_call(
        blend_kernel,
        out_shape=jax.ShapeDtypeStruct((rows, width), jnp.float32),
        in_specs=[pl.BlockSpec(memory_space=pltpu.VMEM)] * len(operands),
        out_specs=pl.BlockSpec(memory_space=pltpu.VMEM),
        compiler_params=pltpu.CompilerParams(vmem_limit_bytes=16 * 2**20),
        cost_estimate=pl.CostEstimate(
            flops=100 * rows * blend.shape[1] * width,
            bytes_accessed=2 * width * (2 * rows + blend.shape[1]),
            transcendentals=0,
        ),
    )(*operands)


def apply_plain(held, gate, up, down):
    pieces = [piece for arrived in held for piece in arrived]
    rows = jnp.concatenate(pieces, axis=0)
    total = 0.0
    for n in range(2):
        left = jnp.dot(rows, gate[n], preferred_element_type=jnp.float32)
        right = jnp.dot(rows, up[n], preferred_element_type=jnp.float32)
        hidden = (jax.nn.silu(left) * right).astype(jnp.bfloat16)
        total = total + jnp.dot(hidden, down[n], preferred_element_type=jnp.float32)
    return jnp.split(total.astype(jnp.bfloat16), len(pieces), axis=0)


def pick_plain(chip, block, width, experts, capacity, routing=None):
    if routing:
        lanes = jnp.pad(mixing_table(*routing, experts), ((0, 0), (0, -experts % 128)))
        block = jnp.concatenate([block, lanes], axis=1)
    placing, blend = slots_of(block[:, width : width + experts], capacity, chip)
    found = pick(placing, block[:, :width]).astype(jnp.bfloat16)
    outs = jnp.split(found, PLANE, axis=0) + [blend]
    return outs + [block] if routing else outs


def local(
    tokens, route_ids, route_gates, gate_weight, up_weight, down_weight, kv_pages, page_target
):
    tok_rows, width = tokens.shape
    chosen = route_ids.shape[1]
    owners = lax.axis_size("expert")
    experts = owners // 2
    planes = experts // PLANE
    stride = 2 * PLANE
    capacity = min(tok_rows, 5 * tok_rows * chosen // (4 * experts))
    chip = lax.axis_index("expert") // 2
    whole = capacity % 8 == 0 and width % 2048 == 0
    choose, work = (pick_pieces, apply) if whole else (pick_plain, apply_plain)
    weights = (gate_weight, up_weight, down_weight)
    group = 2
    swapped, blends, got, outs = [], [], [], []
    outgoing = sort_pages(kv_pages, page_target)
    block = tokens
    for s in range(planes):
        if s:
            *pieces, blend = choose(chip, block, width, experts, capacity)
        else:
            *pieces, blend, block = choose(
                chip, tokens, width, experts, capacity, (route_ids, route_gates)
            )
        blends.append(blend)
        if s < 3:
            swapped.append(send(after(weights[s], *swapped, block), flip=1))
        for j in range(1, PLANE):
            piece = after(pieces[j], got[s - 1][j]) if s else pieces[j]
            pieces[j] = send(piece, flip=2 * j)
        got.append(pieces)
        if s + 1 < planes:
            block = send(block, step=stride)

    for first in range(0, planes, group):
        held = [list(pieces) for pieces in got[first : first + group]]
        held[0][0] = after(held[0][0], *outs)
        outs.extend(work(held, *zip(weights, swapped)))

    arrived = exchange(after(outgoing, block))
    order = list(range(1, planes)) + [0]
    sent, landed = {}, got[-1][1:]
    for s in order:
        mine = outs[s * PLANE : (s + 1) * PLANE]
        sent[s] = [mine[0]]
        for j in range(1, PLANE):
            waits = [landed[-3 if s == 1 else -4]] + ([arrived] if s == order[1] else [])
            landed.append(send(after(mine[j], *waits), flip=2 * j))
            sent[s].append(landed[-1])
    handed = place_pages(arrived, kv_pages.shape)
    sent[1][0] = after(sent[1][0], outs[-1])
    total = None
    for s in order:
        if whole and s not in (1, 0):
            part = blend_pieces(blends[s], sent[s], [])
        else:
            part = jnp.dot(
                blends[s], jnp.concatenate(sent[s], axis=0), preferred_element_type=jnp.float32
            )
        if total is not None:
            part = part + send(total, step=stride).astype(jnp.float32)
        total = part.astype(jnp.bfloat16)
    return (total, handed)


def solution(mesh):
    placed = (
        P(("groups", "expert"), None),
        P(("groups", "expert"), None),
        P(("groups", "expert"), None),
        P(None, "expert"),
        P(None, "expert"),
        P("expert", None),
        P(("groups", "expert"), None, None),
        P(("groups", "expert")),
    )
    return jax.shard_map(
        local,
        mesh=mesh,
        in_specs=placed,
        out_specs=(P(("groups", "expert"), None), P(("groups", "expert"), None, None)),
        check_vma=False,
    )
```
